512 devices in a mesh: rep: 4 (over x_lo, core), ty: 8 (over x_hi, y), tx: 16 (over z).
Axes of the slice: x: 4 (x_hi: 2, x_lo: 2; x = x_hi * 2 + x_lo), y: 4, z: 16, core: 2. Of those that a mesh axis runs over, the one named last changes fastest.
Arguments:
- latent: bfloat16 [16, 16, 32, 3072], P('tx', 'ty', None, 'rep'), may hold values from -6 to 6
- in_weight: bfloat16 [3072, 1920], P(('rep', 'tx')), may hold values from -0.109375 to 0.109375
- qkv_weight: bfloat16 [1920, 3072], P('tx', 'rep'), may hold values from -2 to 2
- out_weight: bfloat16 [1024, 1920], P('rep', 'tx'), may hold values from -0.1875 to 0.1875
- norm_gain: bfloat16 [1920], replicated, may hold values from 0.099609375 to 1.8984375
- extents: int32 [8, 16, 4], P('ty', 'tx'), may hold values from 1 to 4, as said below
Outputs:
- block_out: bfloat16 [16, 64, 128, 1920], P('rep', 'ty', 'tx')
The draws below stay inside these ranges and needn't reach their ends.
Inputs may be any that keep to these rules, and one draw needn't show every extreme that they name: `extents`: each entry is a reach in fine cells; some tile reaches 4 on every side and some tile reaches 1 on every side.
All inputs are finite; a program needn't handle non-finite values.
Results may differ from the reference program's by a relative error of at most 0.04.
Values may be sent and summed in bfloat16 or wider, within the bound.
No kernel may reach another device: no remote copies, remote signals or barrier semaphores. Data moves between devices by JAX's collectives and lax.ppermute only.
A program may use at most 128 MiB of HBM per device.

```python
import jax
import jax.numpy as jnp
from jax import lax

C1 = 3072
D2 = 1920
HD = 64
HEADS = 16
U = 4
FT = 4
R = 4
F = 16
H1 = 16
W1 = 32
TH = 8
TW = 8
H = 64
W = 128
N_REP = 4
N_TY = 8
N_TX = 16


def draw_qkv_weight(key, part):
    key = jax.random.fold_in(key, 7)
    base = jax.random.normal(key, (D2, HEADS, 3, HD), jnp.float32) * D2 ** (-0.5)
    base = jnp.clip(base, -2.0, 2.0)
    return base.reshape(D2, HEADS * 3 * HD).astype(jnp.bfloat16)


def draw_extents(key, part):
    key = jax.random.fold_in(key, 11)
    values = jax.random.randint(key, (N_TY, N_TX, 4), 1, R + 1)
    values = values.at[0, 0, :].set(R)
    values = values.at[N_TY - 1, N_TX - 1, :].set(1)
    return values.astype(jnp.int32)


def block_scale(key, shape, split, low, largest):
    level = 1.0
    for dim, blocks in split:
        draws = jax.random.uniform(jax.random.fold_in(jax.random.fold_in(key, 6), dim), (blocks,), jnp.float32, low / len(split), largest / len(split))
        level = level * jnp.repeat(jnp.exp(draws), shape[dim] // blocks).reshape((-1,) + (1,) * (len(shape) - 1 - dim))
    return level


def centred(stream_key, shape, deviation, bound, pieces=(), kind=jnp.bfloat16):
    result = deviation * jax.random.normal(stream_key, shape, jnp.float32)
    if pieces:
        result = result * block_scale(stream_key, shape, pieces, -0.22, 0.18)
    return jnp.clip(result, -bound, bound).astype(kind)


def setup_inputs(seed: int = 0) -> dict:
    seeds = jax.random.split(jax.random.key(seed), 7)
    return {
        "latent": centred(seeds[0], (F, H1, W1, C1), 1.0, 6.0, ((0, 16), (1, 8), (3, 4))),
        "in_weight": centred(seeds[1], (C1, D2), C1 ** -0.5, 0.109375, ((0, 64),)),
        "qkv_weight": draw_qkv_weight(jax.random.fold_in(seeds[6], 71), 0),
        "out_weight": centred(seeds[3], (HEADS * HD, D2), (HEADS * HD) ** -0.5, 0.1875, ((0, 4), (1, 16))),
        "norm_gain": jnp.clip(1.0 + 0.18 * jax.random.normal(seeds[4], (D2,), jnp.float32), 0.099609375, 1.8984375).astype(jnp.bfloat16),
        "extents": draw_extents(jax.random.fold_in(seeds[6], 71), 0),
    }


precise_mode = lax.Precision.HIGHEST

def interp_matrix(coarse_cells, factor):
    fine_index = jnp.arange(coarse_cells * factor, dtype=jnp.int32)
    coarse_index = fine_index // factor
    offsets = ((fine_index % factor).astype(jnp.float32) + 0.5) / factor - 0.5
    columns = jnp.arange(coarse_cells + 2, dtype=jnp.int32)
    centre = (columns[None, :] == coarse_index[:, None] + 1).astype(jnp.float32) * (1.0 - jnp.abs(offsets))[:, None]
    before = (columns[None, :] == coarse_index[:, None]).astype(jnp.float32) * jnp.maximum(-offsets, 0.0)[:, None]
    following = (columns[None, :] == coarse_index[:, None] + 2).astype(jnp.float32) * jnp.maximum(offsets, 0.0)[:, None]
    return centre + before + following

def window_allowed(row_tile, col_tile, extent, tile_rows, tile_cols, grid_rows, grid_cols):
    local_rows = jnp.arange(tile_rows + 2 * R, dtype=jnp.int32)
    local_cols = jnp.arange(tile_cols + 2 * R, dtype=jnp.int32)
    global_rows = row_tile * tile_rows - R + local_rows
    global_cols = col_tile * tile_cols - R + local_cols
    row_valid = (global_rows >= 0) & (global_rows < grid_rows) & (local_rows >= R - extent[0]) & (local_rows < R + tile_rows + extent[1])
    col_valid = (global_cols >= 0) & (global_cols < grid_cols) & (local_cols >= R - extent[2]) & (local_cols < R + tile_cols + extent[3])
    return row_valid[:, None] & col_valid[None, :]

def window_attend(queries, keys_window, values_window, allowed):
    frame_total = queries.shape[0]
    head_depth = queries.shape[-1]
    groups = frame_total // FT
    flat_query = queries.reshape(groups, -1, head_depth).astype(jnp.float32)
    flat_key = keys_window.reshape(groups, -1, head_depth).astype(jnp.float32)
    flat_value = values_window.reshape(groups, -1, head_depth).astype(jnp.float32)
    scores = jnp.einsum('gqd,gkd->gqk', flat_query, flat_key) * head_depth ** (-0.5)
    key_allowed = jnp.broadcast_to(allowed[None], (FT,) + allowed.shape).reshape(-1)
    scores = jnp.where(key_allowed[None, None, :], scores, -1e+30)
    highest = lax.optimization_barrier(jnp.max(scores, axis=-1, keepdims=True))
    weights = jnp.exp(scores - highest)
    probabilities = (weights / lax.optimization_barrier(jnp.sum(weights, axis=-1, keepdims=True))).astype(jnp.bfloat16)
    mixture = jnp.einsum('gqk,gkd->gqd', probabilities.astype(jnp.float32), flat_value)
    return mixture.astype(jnp.bfloat16).reshape(queries.shape)

def reference(latent, in_weight, qkv_weight, out_weight, norm_gain, extents):
    coarse = jnp.dot(latent.reshape(-1, C1), in_weight, preferred_element_type=jnp.float32).reshape(F, H1, W1, D2)
    padded = jnp.pad(coarse, ((0, 0), (1, 1), (1, 1), (0, 0)), mode='edge')
    row_matrix = interp_matrix(H1, U)
    col_matrix = interp_matrix(W1, U)
    gain_values = norm_gain.astype(jnp.float32)

    def fine_frame(frame_data):
        tall_field = jnp.einsum('hp,pqc->hqc', row_matrix, frame_data, precision=precise_mode)
        fine_field = jnp.einsum('wq,hqc->hwc', col_matrix, tall_field, precision=precise_mode)
        hidden_frame = fine_field.astype(jnp.bfloat16)
        widened = hidden_frame.astype(jnp.float32)
        scale_rows = lax.rsqrt(lax.optimization_barrier(jnp.mean(widened * widened, axis=-1, keepdims=True)) + 1e-06)
        return (hidden_frame, (widened * scale_rows * gain_values).astype(jnp.bfloat16))
    hidden, normed = lax.map(fine_frame, padded)
    head_weights = qkv_weight.reshape(D2, HEADS, 3 * HD).transpose(1, 0, 2)
    flat_normed = normed.reshape(-1, D2)
    zero_index = jnp.int32(0)

    def one_head(weight_slice):
        project = jnp.dot(flat_normed, weight_slice, preferred_element_type=jnp.float32).astype(jnp.bfloat16).reshape(F, H, W, 3, HD)
        queries = project[:, :, :, 0, :]
        keys_pad = jnp.pad(project[:, :, :, 1, :], ((0, 0), (R, R), (R, R), (0, 0)))
        values_pad = jnp.pad(project[:, :, :, 2, :], ((0, 0), (R, R), (R, R), (0, 0)))

        def one_tile(tile_index):
            row_tile = (tile_index // N_TX).astype(jnp.int32)
            col_tile = (tile_index % N_TX).astype(jnp.int32)
            row_start = (row_tile * TH).astype(jnp.int32)
            col_start = (col_tile * TW).astype(jnp.int32)
            query_tile = lax.dynamic_slice(queries, (zero_index, row_start, col_start, zero_index), (F, TH, TW, HD))
            key_tile = lax.dynamic_slice(keys_pad, (zero_index, row_start, col_start, zero_index), (F, TH + 2 * R, TW + 2 * R, HD))
            value_tile = lax.dynamic_slice(values_pad, (zero_index, row_start, col_start, zero_index), (F, TH + 2 * R, TW + 2 * R, HD))
            allowed = window_allowed(row_tile, col_tile, extents[row_tile, col_tile], TH, TW, H, W)
            return window_attend(query_tile, key_tile, value_tile, allowed)
        tiles_out = lax.map(one_tile, jnp.arange(N_TY * N_TX, dtype=jnp.int32))
        return tiles_out.reshape(N_TY, N_TX, F, TH, TW, HD).transpose(2, 0, 3, 1, 4, 5).reshape(F, H, W, HD)
    attended = lax.map(one_head, head_weights)
    per_group = HEADS // N_REP

    def out_frame(frame_index):
        frame_heads = lax.dynamic_index_in_dim(attended, frame_index, 1, keepdims=False)
        running = lax.dynamic_index_in_dim(hidden, frame_index, 0, keepdims=False).reshape(-1, D2).astype(jnp.float32)
        for group in range(N_REP):
            section = frame_heads[group * per_group:(group + 1) * per_group].transpose(1, 2, 0, 3).reshape(H * W, per_group * HD)
            rows_used = out_weight[group * per_group * HD:(group + 1) * per_group * HD]
            partial_sum = jnp.dot(section, rows_used, preferred_element_type=jnp.float32).astype(jnp.bfloat16)
            partial_sum = lax.optimization_barrier(partial_sum)
            running = running + partial_sum.astype(jnp.float32)
        return running.astype(jnp.bfloat16).reshape(H, W, D2)
    return lax.map(out_frame, jnp.arange(F, dtype=jnp.int32))
```

```python
import jax
import jax.numpy as jnp
from jax import lax
from jax.experimental import pallas as pl
from jax.experimental.pallas import tpu as pltpu
from jax.sharding import PartitionSpec as P

HD = 64
U = 4
R = 4
CHUNKS = 16
CHUNK = 120
LANES = 128
WIDE = CHUNKS * LANES
WIDTH = CHUNKS * CHUNK
CELLS = 48
PATCH = 3 * CELLS
NEG = -1e30
F32 = jnp.float32
BF16 = jnp.bfloat16


def call(kernel, out_shape, vmem_mb, **kw):
    return pl.pallas_call(
        kernel,
        out_shape=out_shape,
        compiler_params=pltpu.CompilerParams(vmem_limit_bytes=vmem_mb << 20),
        **kw,
    )


def bridge_kernel(cells_ref, moved_ref, out_ref, weight_ref):
    for t in range(16):
        for b in range(3):
            weight_ref[t * 48 + b * 16 : t * 48 + b * 16 + 16, :] = moved_ref[
                t, 0:16, b * 256 : (b + 1) * 256
            ]
    sums = jnp.dot(cells_ref[...], weight_ref[...], preferred_element_type=F32).astype(BF16)
    for y in range(8):
        for dy in range(3):
            source = min(max(y + dy - 1, 0), 7)
            for r in range(4):
                start = source * 64 + r * 16
                out_ref[r, y, dy] = sums[start : start + 16, :]


def reduce_kernel(parts_ref, gain_ref, coarse_ref, gained_ref):
    for y in range(8):
        total = parts_ref[y].astype(F32)
        for r in range(1, 4):
            total = total + parts_ref[r * 8 + y].astype(F32)
        lanes = slice(y * 256, (y + 1) * 256)
        coarse_ref[:, lanes] = total.astype(BF16)
        gained_ref[:, lanes] = (total * gain_ref[:, lanes]).astype(BF16)


def project_kernel(gained_ref, weights_ref, project_ref, out_weight_ref):
    total = jnp.zeros(project_ref.shape, F32)
    for t in range(CHUNKS):
        total = total + jnp.dot(
            gained_ref[:, t * LANES : (t + 1) * LANES],
            weights_ref[t, 48:176, :],
            preferred_element_type=F32,
        )
    project_ref[...] = total.astype(BF16)
    for t in range(CHUNKS):
        for b in range(6):
            rows = 48 if b < 5 else 16
            out_weight_ref[t, b * 48 : b * 48 + rows, :] = weights_ref[
                t, 0:rows, b * LANES : (b + 1) * LANES
            ]


def axis_weight(fine, cell, low, high):
    near = ((fine + 4) >> 2) - 1
    offset = ((fine + 4) & 3).astype(F32) * 0.25 - 0.375
    before = jnp.clip(near - 1, low, high)
    after = jnp.clip(near + 1, low, high)
    return (
        jnp.where(cell == near, 1.0 - jnp.abs(offset), 0.0)
        + jnp.where(cell == before, jnp.maximum(-offset, 0.0), 0.0)
        + jnp.where(cell == after, jnp.maximum(offset, 0.0), 0.0)
    )


def patch_matrix(frame, fine_row, fine_col, tokens, ty, tx):
    lane = lax.broadcasted_iota(jnp.int32, (tokens, PATCH), 1)
    piece = (lane >= CELLS).astype(jnp.int32) + (lane >= 2 * CELLS).astype(jnp.int32)
    rest = lane - piece * CELLS
    row = ((rest >> 4) << 1) + ((rest >> 1) & 1) - 2
    col = (piece << 1) + (rest & 1) - 2
    weight = axis_weight(fine_row, row, -2 * ty, 15 - 2 * ty) * axis_weight(
        fine_col, col, -2 * tx, 31 - 2 * tx
    )
    return jnp.where(((rest >> 2) & 3) == frame, weight, 0.0).astype(BF16)


def norm_kernel(
    place_ref, left_ref, own_ref, right_ref, keys_ref, query_ref, key_scale_ref, query_scale_ref, bias_ref, hidden_ref
):
    ty, tx = place_ref[0], place_ref[1]
    patch = jnp.concatenate([left_ref[...], own_ref[...], right_ref[...]], axis=0)

    def scale_of(field):
        wide = field.astype(F32)
        return lax.rsqrt(jnp.sum(wide * wide, axis=1, keepdims=True) * (1.0 / WIDTH) + 1e-06)

    token = lax.broadcasted_iota(jnp.int32, (256, PATCH), 0)
    for frame in range(4):
        matrix = patch_matrix(frame, (token >> 4) - R, (token & 15) - R, 256, ty, tx)
        rows = slice(frame * 256, (frame + 1) * 256)
        keys_ref[rows, :] = matrix
        field = jnp.dot(matrix, patch, preferred_element_type=F32).astype(BF16)
        key_scale_ref[rows, :] = jnp.broadcast_to(scale_of(field), (256, LANES))
    matrix = patch_matrix(token >> 6, (token >> 3) & 7, token & 7, 256, ty, tx)
    query_ref[...] = matrix
    hidden = jnp.dot(matrix, patch, preferred_element_type=F32).astype(BF16)
    hidden_ref[...] = hidden
    query_scale_ref[...] = jnp.broadcast_to(scale_of(hidden), (256, LANES))
    place = lax.broadcasted_iota(jnp.int32, (1024, LANES), 0)
    row = ((place >> 4) & 15) - R
    col = (place & 15) - R
    allowed = (
        (row + 8 * ty >= 0)
        & (row + 8 * ty < 64)
        & (row >= -place_ref[2])
        & (row < 8 + place_ref[3])
        & (col + 8 * tx >= 0)
        & (col + 8 * tx < 128)
        & (col >= -place_ref[4])
        & (col < 8 + place_ref[5])
    )
    bias_ref[...] = jnp.where(allowed, 0.0, NEG)


def attend_kernel(
    left_ref, own_ref, right_ref, keys_ref, query_ref, key_scale_ref, query_scale_ref, bias_ref, out_ref
):
    patch = jnp.concatenate([left_ref[0], own_ref[0], right_ref[0]], axis=0)
    fine = jnp.dot(keys_ref[...], patch, preferred_element_type=F32)
    scale = key_scale_ref[...]
    bias = bias_ref[...]
    first = fine[:, 0:128] * scale
    second = fine[:, 128:256] * scale
    third = fine[:, 256:384] * scale
    lane = lax.broadcasted_iota(jnp.int32, (1024, LANES), 1)
    low = lane < HD
    key_0 = jnp.where(low, jnp.where(lane == 0, bias, 0.0), first).astype(BF16)
    value_0 = jnp.where(low, second, 1.0).astype(BF16)
    key_1 = jnp.where(low, third, jnp.where(lane == HD, bias, 0.0)).astype(BF16)
    value_1 = jnp.where(low, 1.0, third).astype(BF16)
    query = jnp.dot(query_ref[...], patch[:, 0:256], preferred_element_type=F32)
    query_scale = query_scale_ref[...] * (HD ** (-0.5) * 1.4426950408889634)
    query_lane = lax.broadcasted_iota(jnp.int32, (256, LANES), 1)
    query_low = query_lane < HD
    turned_0 = pltpu.roll(query[:, 0:128] * query_scale, HD, 1)
    turned_1 = pltpu.roll(query[:, 128:256] * query_scale, HD, 1)
    query_0 = jnp.where(query_low, jnp.where(query_lane == 0, 1.0, 0.0), turned_0).astype(BF16)
    query_1 = jnp.where(query_low, turned_1, jnp.where(query_lane == HD, 1.0, 0.0)).astype(BF16)

    def head(q, k, v):
        scores = lax.dot_general(q, k, (((1,), (1,)), ((), ())), preferred_element_type=F32)
        weights = jnp.exp2(scores - jnp.max(scores, axis=1, keepdims=True)).astype(BF16)
        return jnp.dot(weights, v, preferred_element_type=F32)

    mixed_0 = head(query_0, key_0, value_0)
    mixed_1 = head(query_1, key_1, value_1)
    mixed = jnp.where(query_low, mixed_0 / mixed_0[:, HD : HD + 1], mixed_1 / mixed_1[:, 0:1])
    out_ref[0] = mixed.astype(BF16)


def output_kernel(place_ref, attended_ref, hidden_ref, w0_ref, w1_ref, w2_ref, w3_ref, out_ref):
    rep = place_ref[0]
    weights = (w0_ref, w1_ref, w2_ref, w3_ref)
    groups = [attended_ref[rep ^ k] for k in range(4)]
    chunks = []
    for t in range(0, CHUNKS, 2):
        total = hidden_ref[:, t * LANES : (t + 2) * LANES].astype(F32)
        for k in range(4):
            pair = jnp.concatenate([weights[k][t], weights[k][t + 1]], axis=1)
            total = total + jnp.dot(groups[k], pair, preferred_element_type=F32)
        chunks.append(total[:, 0:LANES])
        chunks.append(total[:, LANES : 2 * LANES])
    lane = lax.broadcasted_iota(jnp.int32, (256, LANES), 1)
    for j in range(15):
        here, shift = chunks[j], (LANES - 8 * j) % LANES
        if shift:
            here = pltpu.roll(here, shift, 1)
        after = pltpu.roll(chunks[j + 1], CHUNK - 8 * j, 1)
        out_ref[:, j * LANES : (j + 1) * LANES] = jnp.where(lane < CHUNK - 8 * j, here, after).astype(BF16)


def body(latent, in_weight, qkv_weight, out_weight, norm_gain, extents):
    ty = lax.axis_index("ty")
    tx = lax.axis_index("tx")
    rep = lax.axis_index("rep")
    smem = pl.BlockSpec(memory_space=pltpu.SMEM)

    out_rows = jnp.pad(out_weight, ((0, 32), (0, LANES - CHUNK))).reshape(6, 48, LANES)
    shard = jnp.concatenate(
        [out_rows.transpose(1, 0, 2).reshape(48, 768), qkv_weight, jnp.zeros((8, 768), BF16)], axis=0
    )
    gathered = lax.all_gather(shard, "tx", axis=0)

    source = lax.broadcasted_iota(jnp.int32, (WIDTH, 256), 0)
    target = lax.broadcasted_iota(jnp.int32, (WIDTH, 256), 1)
    inside = target & 127
    pick = ((inside < CHUNK) & (source == ty * 240 + (target >> 7) * CHUNK + inside)).astype(BF16)
    columns = jnp.dot(in_weight, pick, preferred_element_type=F32).astype(BF16)
    columns = columns.reshape(3, 16, 256).transpose(1, 0, 2).reshape(1, 16, 768)
    tiles = latent.reshape(2, 16, 2, 768).transpose(1, 0, 2, 3).reshape(16, 4, 768)
    message = jnp.concatenate([jnp.broadcast_to(columns, (16, 16, 768)), tiles], axis=1)
    moved = lax.all_to_all(message, "tx", split_axis=0, concat_axis=0, tiled=True)
    cells = moved[:, 16:20, :].reshape(1, 64, 768)
    cells = lax.all_to_all(jnp.broadcast_to(cells, (8, 64, 768)), "ty", split_axis=0, concat_axis=0, tiled=True)
    sums = call(
        bridge_kernel,
        jax.ShapeDtypeStruct((4, 8, 3, 16, 256), BF16),
        16,
        scratch_shapes=[pltpu.VMEM((768, 256), BF16)],
    )(cells.reshape(512, 768), moved)
    parts = lax.all_to_all(
        sums.reshape(32, CELLS, 256), ("rep", "ty"), split_axis=0, concat_axis=0, tiled=True
    )
    gain = jnp.pad(norm_gain.astype(F32).reshape(CHUNKS, CHUNK), ((0, 0), (0, LANES - CHUNK))).reshape(1, WIDE)
    coarse, gained = call(
        reduce_kernel, [jax.ShapeDtypeStruct((CELLS, WIDE), BF16)] * 2, 16
    )(parts, gain)

    count = lax.axis_size("tx")
    to_right = [(i, i + 1) for i in range(count - 1)]
    to_left = [(i + 1, i) for i in range(count - 1)]
    coarse_left = lax.ppermute(coarse, "tx", to_right)
    coarse_right = lax.ppermute(coarse, "tx", to_left)
    gained = lax.all_gather(gained, "rep", axis=0, tiled=True)
    project, own_rows = call(
        project_kernel,
        [jax.ShapeDtypeStruct((4 * CELLS, 768), BF16), jax.ShapeDtypeStruct((CHUNKS, 256, LANES), BF16)],
        32,
    )(gained, gathered)
    project = lax.all_to_all(
        project.reshape(4, CELLS, 768), "rep", split_axis=0, concat_axis=0, tiled=True
    )
    project_left = lax.ppermute(project, "tx", to_right)
    project_right = lax.ppermute(project, "tx", to_left)

    far_rows = lax.ppermute(own_rows, "rep", [(i, i ^ 2) for i in range(4)])
    near_rows = lax.ppermute(own_rows, "rep", [(i, i ^ 1) for i in range(4)])
    last_rows = lax.ppermute(far_rows, "rep", [(i, i ^ 1) for i in range(4)])

    place = jnp.concatenate([jnp.stack([ty, tx]).astype(jnp.int32), extents.reshape(4)])
    vmem = pl.BlockSpec(memory_space=pltpu.VMEM)
    keys, query, key_scale, query_scale, bias, hidden = call(
        norm_kernel,
        [
            jax.ShapeDtypeStruct((1024, PATCH), BF16),
            jax.ShapeDtypeStruct((256, PATCH), BF16),
            jax.ShapeDtypeStruct((1024, LANES), F32),
            jax.ShapeDtypeStruct((256, LANES), F32),
            jax.ShapeDtypeStruct((1024, LANES), F32),
            jax.ShapeDtypeStruct((256, WIDE), BF16),
        ],
        32,
        in_specs=[smem, vmem, vmem, vmem],
        out_specs=[vmem] * 6,
    )(place, coarse_left, coarse, coarse_right)

    piece = pl.BlockSpec((1, CELLS, 384), lambda p: (p // 2, 0, p % 2))

    def whole(shape):
        return pl.BlockSpec(shape, lambda p: (0, 0))

    attended = call(
        attend_kernel,
        jax.ShapeDtypeStruct((4, 256, 256), BF16),
        32,
        grid=(8,),
        in_specs=[
            piece,
            piece,
            piece,
            whole((1024, PATCH)),
            whole((256, PATCH)),
            whole((1024, LANES)),
            whole((256, LANES)),
            whole((1024, LANES)),
        ],
        out_specs=pl.BlockSpec((1, 256, LANES), lambda p: (p // 2, 0, p % 2)),
    )(project_left, project, project_right, keys, query, key_scale, query_scale, bias)

    result = call(
        output_kernel,
        jax.ShapeDtypeStruct((256, WIDTH), BF16),
        32,
        in_specs=[smem] + [vmem] * 6,
        out_specs=vmem,
    )(rep.astype(jnp.int32).reshape(1), attended, hidden, own_rows, near_rows, far_rows, last_rows)
    return result.reshape(4, 8, 8, WIDTH)


def solution(mesh):
    return jax.shard_map(
        body,
        mesh=mesh,
        in_specs=(
            P("tx", "ty", None, "rep"),
            P(("rep", "tx"), None),
            P("tx", "rep"),
            P("rep", "tx"),
            P(),
            P("ty", "tx", None),
        ),
        out_specs=P("rep", "ty", "tx", None),
        check_vma=False,
    )
```

```python
import jax
import jax.numpy as jnp
from jax import lax
from jax.experimental import pallas as pl
from jax.experimental.pallas import tpu as pltpu
from jax.sharding import PartitionSpec as P

HD = 64
U = 4
R = 4
CHUNKS = 16
CHUNK = 120
LANES = 128
WIDE = CHUNKS * LANES
WIDTH = CHUNKS * CHUNK
CELLS = 48
PATCH = 3 * CELLS
NEG = -1e30
F32 = jnp.float32
BF16 = jnp.bfloat16


def call(kernel, out_shape, vmem_mb, mflops, kbytes, **kw):
    return pl.pallas_call(
        kernel,
        out_shape=out_shape,
        compiler_params=pltpu.CompilerParams(vmem_limit_bytes=vmem_mb << 20),
        cost_estimate=pl.CostEstimate(flops=mflops * 10**6, bytes_accessed=kbytes * 1000, transcendentals=0),
        **kw,
    )


def pack_kernel(place_ref, latent_ref, weight_ref, out_ref):
    weight = weight_ref[...].astype(F32)
    block = slice_of(weight, 0)
    for ty in range(1, 8):
        block = jnp.where(place_ref[0] == ty, slice_of(weight, ty), block)
    chunks = [block[:, 0:LANES], block[:, LANES : 2 * LANES]]
    latent = latent_ref[0].astype(F32)
    for t in range(16):
        cells = jnp.concatenate([latent[0, 2 * t : 2 * t + 2], latent[1, 2 * t : 2 * t + 2]], axis=0)
        cells = [cells[:, b * LANES : (b + 1) * LANES] for b in range(6)]
        out_ref[t] = jnp.concatenate(chunks + cells, axis=0).astype(BF16)


def slice_of(rows, ty):
    lane = lax.broadcasted_iota(jnp.int32, (rows.shape[0], LANES), 1)
    chunks = []
    for t in (2 * ty, 2 * ty + 1):
        tile, shift = divmod(t * CHUNK, LANES)
        first = rows[:, tile * LANES : (tile + 1) * LANES]
        if shift:
            first = pltpu.roll(first, LANES - shift, 1)
        if shift > LANES - CHUNK:
            second = rows[:, (tile + 1) * LANES : (tile + 2) * LANES]
            second = pltpu.roll(second, LANES - shift, 1)
            first = jnp.where(lane < LANES - shift, first, second)
        chunks.append(jnp.where(lane < CHUNK, first, 0.0))
    return jnp.concatenate(chunks, axis=1)


def spread_kernel(moved_ref, out_ref):
    cells = moved_ref[:, 96:120, :].astype(F32)
    cells = jnp.concatenate(
        [cells[:, b * 4 : b * 4 + 4, :].reshape(64, LANES) for b in range(6)], axis=1
    ).astype(BF16)
    for ty in range(8):
        out_ref[ty] = cells


def bridge_kernel(cells_ref, moved_ref, out_ref):
    weight = jnp.concatenate(
        [moved_ref[:, c * 48 : c * 48 + 48, :].reshape(768, LANES) for c in range(2)], axis=1
    )
    sums = jnp.dot(cells_ref[...], weight, preferred_element_type=F32).astype(BF16)
    for y in range(8):
        for dy in range(3):
            source = min(max(y + dy - 1, 0), 7)
            for r in range(4):
                start = source * 64 + r * 16
                out_ref[r, y, dy] = sums[start : start + 16, :]


def reduce_kernel(parts_ref, gain_ref, coarse_ref, gained_ref):
    for y in range(8):
        total = parts_ref[y].astype(F32)
        for r in range(1, 4):
            total = total + parts_ref[r * 8 + y].astype(F32)
        lanes = slice(y * 256, (y + 1) * 256)
        coarse_ref[:, lanes] = total.astype(BF16)
        gained_ref[:, lanes] = (total * gain_ref[:, lanes]).astype(BF16)


def project_kernel(gained_ref, weights_ref, project_ref, out_weight_ref, total_ref):
    step = pl.program_id(0)
    total = jnp.zeros(total_ref.shape, F32)
    for t in range(4):
        total = total + jnp.dot(
            gained_ref[:, t * LANES : t * LANES + CHUNK],
            weights_ref[t, 48:168, :],
            preferred_element_type=F32,
        )
        for b in range(6):
            rows = 48 if b < 5 else 16
            out_weight_ref[t, b * 48 : b * 48 + rows, :] = weights_ref[
                t, 0:rows, b * LANES : (b + 1) * LANES
            ]

    @pl.when(step == 0)
    def _():
        total_ref[...] = total

    @pl.when(step > 0)
    def _():
        total_ref[...] += total

    @pl.when(step == 3)
    def _():
        project_ref[...] = total_ref[...].astype(BF16)


def tie_kernel(rows_ref, after_ref, out_ref):
    pass


def tie(rows, after):
    anywhere = pl.BlockSpec(memory_space=pl.ANY)
    return call(
        tie_kernel,
        jax.ShapeDtypeStruct(rows.shape, rows.dtype),
        4,
        1,
        1,
        in_specs=[anywhere, anywhere],
        out_specs=anywhere,
        input_output_aliases={0: 0},
    )(rows, after)


def axis_weight(fine, cell, low, high):
    near = ((fine + 4) >> 2) - 1
    offset = ((fine + 4) & 3).astype(F32) * 0.25 - 0.375
    before = jnp.clip(near - 1, low, high)
    after = jnp.clip(near + 1, low, high)
    return (
        jnp.where(cell == near, 1.0 - jnp.abs(offset), 0.0)
        + jnp.where(cell == before, jnp.maximum(-offset, 0.0), 0.0)
        + jnp.where(cell == after, jnp.maximum(offset, 0.0), 0.0)
    )


def patch_matrix(frame, fine_row, fine_col, tokens, ty, tx):
    lane = lax.broadcasted_iota(jnp.int32, (tokens, PATCH), 1)
    piece = (lane >= CELLS).astype(jnp.int32) + (lane >= 2 * CELLS).astype(jnp.int32)
    rest = lane - piece * CELLS
    row = ((rest >> 4) << 1) + ((rest >> 1) & 1) - 2
    col = (piece << 1) + (rest & 1) - 2
    weight = axis_weight(fine_row, row, -2 * ty, 15 - 2 * ty) * axis_weight(
        fine_col, col, -2 * tx, 31 - 2 * tx
    )
    return jnp.where(((rest >> 2) & 3) == frame, weight, 0.0).astype(BF16)


def norm_kernel(
    place_ref, left_ref, own_ref, right_ref, keys_ref, query_ref, key_scale_ref, query_scale_ref, bias_ref, hidden_ref
):
    ty, tx = place_ref[0], place_ref[1]
    patch = jnp.concatenate([left_ref[...], own_ref[...], right_ref[...]], axis=0)

    def scale_of(field):
        wide = field.astype(F32)
        return lax.rsqrt(jnp.sum(wide * wide, axis=1, keepdims=True) * (1.0 / WIDTH) + 1e-06)

    token = lax.broadcasted_iota(jnp.int32, (256, PATCH), 0)
    for frame in range(4):
        matrix = patch_matrix(frame, (token >> 4) - R, (token & 15) - R, 256, ty, tx)
        rows = slice(frame * 256, (frame + 1) * 256)
        keys_ref[rows, :] = matrix
        field = jnp.dot(matrix, patch, preferred_element_type=F32).astype(BF16)
        key_scale_ref[rows, :] = jnp.broadcast_to(scale_of(field), (256, LANES))
    matrix = patch_matrix(token >> 6, (token >> 3) & 7, token & 7, 256, ty, tx)
    query_ref[...] = matrix
    hidden = jnp.dot(matrix, patch, preferred_element_type=F32).astype(BF16)
    hidden_ref[...] = hidden
    query_scale_ref[...] = jnp.broadcast_to(scale_of(hidden), (256, LANES))
    place = lax.broadcasted_iota(jnp.int32, (1024, LANES), 0)
    row = ((place >> 4) & 15) - R
    col = (place & 15) - R
    allowed = (
        (row + 8 * ty >= 0)
        & (row + 8 * ty < 64)
        & (row >= -place_ref[2])
        & (row < 8 + place_ref[3])
        & (col + 8 * tx >= 0)
        & (col + 8 * tx < 128)
        & (col >= -place_ref[4])
        & (col < 8 + place_ref[5])
    )
    lane = lax.broadcasted_iota(jnp.int32, (1024, LANES), 1)
    bias_ref[...] = jnp.where(((lane & (HD - 1)) == 0) & ~allowed, NEG, 0.0)


def attend_kernel(
    left_ref, own_ref, right_ref, keys_ref, query_ref, key_scale_ref, query_scale_ref, bias_ref, out_ref
):
    patch = jnp.concatenate([left_ref[0], own_ref[0], right_ref[0]], axis=0)
    fine = jnp.dot(keys_ref[...], patch, preferred_element_type=F32)
    scale = key_scale_ref[...]
    bias = bias_ref[...]
    first = fine[:, 0:128] * scale
    second = fine[:, 128:256] * scale
    third = fine[:, 256:384] * scale
    lane = lax.broadcasted_iota(jnp.int32, (1024, LANES), 1)
    low = lane < HD
    key_0 = jnp.where(low, bias, first).astype(BF16)
    value_0 = jnp.where(low, second, 1.0).astype(BF16)
    key_1 = jnp.where(low, third, bias).astype(BF16)
    value_1 = jnp.where(low, 1.0, third).astype(BF16)
    query = jnp.dot(query_ref[...], patch[:, 0:256], preferred_element_type=F32)
    query_scale = query_scale_ref[...] * (HD ** (-0.5) * 1.4426950408889634)
    query_lane = lax.broadcasted_iota(jnp.int32, (256, LANES), 1)
    query_low = query_lane < HD
    turned_0 = pltpu.roll(query[:, 0:128] * query_scale, HD, 1)
    turned_1 = pltpu.roll(query[:, 128:256] * query_scale, HD, 1)
    query_0 = jnp.where(query_low, jnp.where(query_lane == 0, 1.0, 0.0), turned_0).astype(BF16)
    query_1 = jnp.where(query_low, turned_1, jnp.where(query_lane == HD, 1.0, 0.0)).astype(BF16)

    def head(q, k, v):
        scores = lax.dot_general(q, k, (((1,), (1,)), ((), ())), preferred_element_type=F32)
        weights = jnp.exp2(scores - jnp.max(scores, axis=1, keepdims=True)).astype(BF16)
        return jnp.dot(weights, v, preferred_element_type=F32)

    mixed_0 = head(query_0, key_0, value_0)
    mixed_1 = head(query_1, key_1, value_1)
    mixed = jnp.where(query_low, mixed_0 / mixed_0[:, HD : HD + 1], mixed_1 / mixed_1[:, 0:1])
    out_ref[0] = mixed.astype(BF16)


def times_rows(group, rows, t):
    pair = jnp.concatenate([rows[t], rows[t + 1]], axis=1)
    return jnp.dot(group, pair, preferred_element_type=F32)


def partial_kernel(place_ref, attended_ref, hidden_ref, own_ref, near_ref, far_ref, out_ref):
    rep = place_ref[0]
    groups = [attended_ref[rep ^ k] for k in range(3)]
    for t in range(0, CHUNKS, 2):
        lanes = slice(t * LANES, (t + 2) * LANES)
        total = hidden_ref[:, lanes].astype(F32)
        for group, rows in zip(groups, (own_ref, near_ref, far_ref)):
            total = total + times_rows(group, rows, t)
        out_ref[:, lanes] = total


def output_kernel(place_ref, attended_ref, total_ref, last_ref, out_ref):
    group = attended_ref[place_ref[0] ^ 3]
    chunks = []
    for t in range(0, CHUNKS, 2):
        total = total_ref[:, t * LANES : (t + 2) * LANES] + times_rows(group, last_ref, t)
        chunks.append(total[:, 0:LANES])
        chunks.append(total[:, LANES : 2 * LANES])
    lane = lax.broadcasted_iota(jnp.int32, (256, LANES), 1)
    for j in range(15):
        here, shift = chunks[j], (LANES - 8 * j) % LANES
        if shift:
            here = pltpu.roll(here, shift, 1)
        after = pltpu.roll(chunks[j + 1], CHUNK - 8 * j, 1)
        out_ref[:, j * LANES : (j + 1) * LANES] = jnp.where(lane < CHUNK - 8 * j, here, after).astype(BF16)


def body(latent, in_weight, qkv_weight, out_weight, norm_gain, extents):
    ty = lax.axis_index("ty")
    tx = lax.axis_index("tx")
    rep = lax.axis_index("rep")
    smem = pl.BlockSpec(memory_space=pltpu.SMEM)

    out_rows = jnp.pad(out_weight, ((0, 32), (0, LANES - CHUNK))).reshape(6, 48, LANES)
    shard = jnp.concatenate([out_rows.transpose(1, 0, 2).reshape(48, 768), qkv_weight], axis=0)
    gathered = lax.all_gather(shard, "tx", axis=0)

    vmem = pl.BlockSpec(memory_space=pltpu.VMEM)
    message = call(
        pack_kernel,
        jax.ShapeDtypeStruct((16, 120, LANES), BF16),
        16,
        10,
        500,
        in_specs=[smem, vmem, vmem],
        out_specs=vmem,
    )(ty.astype(jnp.int32).reshape(1), latent, in_weight)
    moved = lax.all_to_all(message, "tx", split_axis=0, concat_axis=0, tiled=True)
    cells = call(spread_kernel, jax.ShapeDtypeStruct((8, 64, 768), BF16), 16, 10, 1500)(moved)
    cells = lax.all_to_all(cells, "ty", split_axis=0, concat_axis=0, tiled=True)
    sums = call(bridge_kernel, jax.ShapeDtypeStruct((4, 8, 3, 16, 256), BF16), 16, 800, 2000)(
        cells.reshape(512, 768), moved
    )
    parts = lax.all_to_all(
        sums.reshape(32, CELLS, 256), ("rep", "ty"), split_axis=0, concat_axis=0, tiled=True
    )
    gain = jnp.pad(norm_gain.astype(F32).reshape(CHUNKS, CHUNK), ((0, 0), (0, LANES - CHUNK))).reshape(1, WIDE)
    coarse, gained = call(
        reduce_kernel, [jax.ShapeDtypeStruct((CELLS, WIDE), BF16)] * 2, 16, 100, 2000
    )(parts, gain)

    count = lax.axis_size("tx")
    to_right = [(i, i + 1) for i in range(count - 1)]
    to_left = [(i + 1, i) for i in range(count - 1)]
    coarse_left = lax.ppermute(coarse, "tx", to_right)
    coarse_right = lax.ppermute(coarse, "tx", to_left)
    gained = lax.all_gather(gained, "rep", axis=0, tiled=True)
    project, own_rows = call(
        project_kernel,
        [jax.ShapeDtypeStruct((4 * CELLS, 768), BF16), jax.ShapeDtypeStruct((CHUNKS, 256, LANES), BF16)],
        32,
        1000,
        6000,
        grid=(4,),
        in_specs=[
            pl.BlockSpec((4 * CELLS, 4 * LANES), lambda k: (0, k)),
            pl.BlockSpec((4, 168, 768), lambda k: (k, 0, 0)),
        ],
        out_specs=[
            pl.BlockSpec((4 * CELLS, 768), lambda k: (0, 0)),
            pl.BlockSpec((4, 256, LANES), lambda k: (k, 0, 0)),
        ],
        scratch_shapes=[pltpu.VMEM((4 * CELLS, 768), F32)],
    )(gained, gathered)
    project = lax.all_to_all(
        project.reshape(4, CELLS, 768), "rep", split_axis=0, concat_axis=0, tiled=True
    )
    own_rows = tie(own_rows, project)
    project_left = lax.ppermute(project, "tx", to_right)
    project_right = lax.ppermute(project, "tx", to_left)

    far_rows = lax.ppermute(own_rows, "rep", [(i, i ^ 2) for i in range(4)])
    near_rows = lax.ppermute(own_rows, "rep", [(i, i ^ 1) for i in range(4)])

    place = jnp.concatenate([jnp.stack([ty, tx]).astype(jnp.int32), extents.reshape(4)])
    keys, query, key_scale, query_scale, bias, hidden = call(
        norm_kernel,
        [
            jax.ShapeDtypeStruct((1024, PATCH), BF16),
            jax.ShapeDtypeStruct((256, PATCH), BF16),
            jax.ShapeDtypeStruct((1024, LANES), F32),
            jax.ShapeDtypeStruct((256, LANES), F32),
            jax.ShapeDtypeStruct((1024, LANES), F32),
            jax.ShapeDtypeStruct((256, WIDE), BF16),
        ],
        32,
        2000,
        8000,
        in_specs=[smem, vmem, vmem, vmem],
        out_specs=[vmem] * 6,
    )(place, coarse_left, coarse, coarse_right)

    def whole(shape):
        return pl.BlockSpec(shape, lambda p: (0, 0))

    piece = pl.BlockSpec((1, CELLS, 384), lambda p: (p // 2, 0, p % 2))
    attended = call(
        attend_kernel,
        jax.ShapeDtypeStruct((4, 256, 256), BF16),
        32,
        10000,
        40000,
        grid=(8,),
        in_specs=[
            piece,
            piece,
            piece,
            whole((1024, PATCH)),
            whole((256, PATCH)),
            whole((1024, LANES)),
            whole((256, LANES)),
            whole((1024, LANES)),
        ],
        out_specs=pl.BlockSpec((1, 256, LANES), lambda p: (p // 2, 0, p % 2)),
    )(project_left, project, project_right, keys, query, key_scale, query_scale, bias)

    far_rows = tie(far_rows, attended)
    last_rows = lax.ppermute(far_rows, "rep", [(i, i ^ 1) for i in range(4)])
    group = rep.astype(jnp.int32).reshape(1)
    total = call(
        partial_kernel,
        jax.ShapeDtypeStruct((256, WIDE), F32),
        32,
        1000,
        6000,
        in_specs=[smem] + [vmem] * 5,
        out_specs=vmem,
    )(group, attended, hidden, own_rows, near_rows, far_rows)
    result = call(
        output_kernel,
        jax.ShapeDtypeStruct((256, WIDTH), BF16),
        32,
        300,
        3000,
        in_specs=[smem] + [vmem] * 3,
        out_specs=vmem,
    )(group, attended, total, last_rows)
    return result.reshape(4, 8, 8, WIDTH)


def solution(mesh):
    return jax.shard_map(
        body,
        mesh=mesh,
        in_specs=(
            P("tx", "ty", None, "rep"),
            P(("rep", "tx"), None),
            P("tx", "rep"),
            P("rep", "tx"),
            P(),
            P("ty", "tx", None),
        ),
        out_specs=P("rep", "ty", "tx", None),
        check_vma=False,
    )
```

```python
import jax
import jax.numpy as jnp
from jax import lax
from jax.experimental import pallas as pl
from jax.experimental.pallas import tpu as pltpu
from jax.sharding import PartitionSpec as P

HD = 64
U = 4
R = 4
CHUNKS = 16
CHUNK = 120
LANES = 128
WIDE = CHUNKS * LANES
WIDTH = CHUNKS * CHUNK
CELLS = 48
PATCH = 3 * CELLS
NEG = -1e30
F32 = jnp.float32
BF16 = jnp.bfloat16


def call(kernel, out_shape, vmem_mb, mflops, kbytes, **kw):
    return pl.pallas_call(
        kernel,
        out_shape=out_shape,
        compiler_params=pltpu.CompilerParams(vmem_limit_bytes=vmem_mb << 20),
        cost_estimate=pl.CostEstimate(flops=mflops * 10**6, bytes_accessed=kbytes * 1000, transcendentals=0),
        **kw,
    )


def start_kernel(
    place_ref, latent_hbm, weight_hbm, qkv_hbm, out_weight_hbm, message_ref, shard_ref, latent_ref, weight_ref, qkv_ref, out_weight_ref, sems
):
    copies = [
        pltpu.make_async_copy(source, target, sems.at[i])
        for i, (source, target) in enumerate(
            (
                (out_weight_hbm, out_weight_ref),
                (qkv_hbm, qkv_ref),
                (weight_hbm, weight_ref),
                (latent_hbm, latent_ref),
            )
        )
    ]
    for copy in copies:
        copy.start()
    copies[0].wait()
    rows = out_weight_ref[...].astype(F32)
    rows = jnp.concatenate([rows, jnp.zeros((LANES - CHUNK, 256), F32)], axis=0).T
    rows = jnp.concatenate([rows, jnp.zeros((32, LANES), F32)], axis=0)
    rows = jnp.concatenate([rows[b * 48 : (b + 1) * 48] for b in range(6)], axis=1)
    shard_ref[128:176, :] = rows.astype(BF16)
    copies[1].wait()
    shard_ref[0:128, :] = jnp.concatenate([qkv_ref[...], jnp.zeros((8, 768), BF16)], axis=0)
    copies[2].wait()
    weight = weight_ref[...].astype(F32)
    block = slice_of(weight, 0)
    for ty in range(1, 8):
        block = jnp.where(place_ref[0] == ty, slice_of(weight, ty), block)
    chunks = [block[:, 0:LANES], block[:, LANES : 2 * LANES]]
    copies[3].wait()
    latent = latent_ref[0].astype(F32)
    for t in range(16):
        cells = jnp.concatenate([latent[0, 2 * t : 2 * t + 2], latent[1, 2 * t : 2 * t + 2]], axis=0)
        cells = [cells[:, b * LANES : (b + 1) * LANES] for b in range(6)]
        message_ref[t] = jnp.concatenate(chunks + cells, axis=0).astype(BF16)


def slice_of(rows, ty):
    lane = lax.broadcasted_iota(jnp.int32, (rows.shape[0], LANES), 1)
    chunks = []
    for t in (2 * ty, 2 * ty + 1):
        tile, shift = divmod(t * CHUNK, LANES)
        first = rows[:, tile * LANES : (tile + 1) * LANES]
        if shift:
            first = pltpu.roll(first, LANES - shift, 1)
        if shift > LANES - CHUNK:
            second = rows[:, (tile + 1) * LANES : (tile + 2) * LANES]
            second = pltpu.roll(second, LANES - shift, 1)
            first = jnp.where(lane < LANES - shift, first, second)
        chunks.append(jnp.where(lane < CHUNK, first, 0.0))
    return jnp.concatenate(chunks, axis=1)


def spread_kernel(moved_ref, out_ref):
    cells = moved_ref[:, 96:120, :].astype(F32)
    cells = jnp.concatenate(
        [cells[:, b * 4 : b * 4 + 4, :].reshape(64, LANES) for b in range(6)], axis=1
    ).astype(BF16)
    for ty in range(8):
        out_ref[ty] = cells


def bridge_kernel(cells_ref, moved_ref, out_ref):
    weight = jnp.concatenate(
        [moved_ref[:, c * 48 : c * 48 + 48, :].reshape(768, LANES) for c in range(2)], axis=1
    )
    sums = jnp.dot(cells_ref[...], weight, preferred_element_type=F32).astype(BF16)
    for y in range(8):
        for dy in range(3):
            source = min(max(y + dy - 1, 0), 7)
            for r in range(4):
                start = source * 64 + r * 16
                out_ref[r, y, dy] = sums[start : start + 16, :]


def reduce_kernel(parts_ref, gain_ref, coarse_ref, gained_ref):
    for y in range(8):
        total = parts_ref[y].astype(F32)
        for r in range(1, 4):
            total = total + parts_ref[r * 8 + y].astype(F32)
        lanes = slice(y * 256, (y + 1) * 256)
        coarse_ref[:, lanes] = total.astype(BF16)
        gained_ref[:, lanes] = (total * gain_ref[:, lanes]).astype(BF16)


def project_kernel(gained_ref, shards_hbm, project_ref, weights_ref, sems):
    copies = []
    for k in range(4):
        part = pl.ds(4 * k, 4)
        copies.append(
            pltpu.make_async_copy(shards_hbm.at[part, pl.ds(0, LANES), :], weights_ref.at[part], sems.at[k])
        )
        copies[k].start()
    total = jnp.zeros(project_ref.shape, F32)
    for k in range(4):
        copies[k].wait()
        total = total + jnp.dot(
            gained_ref[:, k * 512 : (k + 1) * 512],
            weights_ref[4 * k : 4 * k + 4].reshape(512, 768),
            preferred_element_type=F32,
        )
    project_ref[...] = total.astype(BF16)


def rows_kernel(weights_hbm, after_ref, out_ref, weights_ref, sem):
    copy = pltpu.make_async_copy(weights_hbm.at[:, pl.ds(LANES, 48), :], weights_ref, sem)
    copy.start()
    copy.wait()
    for t in range(CHUNKS):
        for b in range(6):
            rows = 48 if b < 5 else 16
            out_ref[t, b * 48 : b * 48 + rows, :] = weights_ref[t, 0:rows, b * LANES : (b + 1) * LANES]


def axis_weight(fine, cell, low, high):
    near = ((fine + 4) >> 2) - 1
    offset = ((fine + 4) & 3).astype(F32) * 0.25 - 0.375
    before = jnp.clip(near - 1, low, high)
    after = jnp.clip(near + 1, low, high)
    return (
        jnp.where(cell == near, 1.0 - jnp.abs(offset), 0.0)
        + jnp.where(cell == before, jnp.maximum(-offset, 0.0), 0.0)
        + jnp.where(cell == after, jnp.maximum(offset, 0.0), 0.0)
    )


def patch_matrix(frame, fine_row, fine_col, tokens, ty, tx):
    lane = lax.broadcasted_iota(jnp.int32, (tokens, PATCH), 1)
    piece = (lane >= CELLS).astype(jnp.int32) + (lane >= 2 * CELLS).astype(jnp.int32)
    rest = lane - piece * CELLS
    row = ((rest >> 4) << 1) + ((rest >> 1) & 1) - 2
    col = (piece << 1) + (rest & 1) - 2
    weight = axis_weight(fine_row, row, -2 * ty, 15 - 2 * ty) * axis_weight(
        fine_col, col, -2 * tx, 31 - 2 * tx
    )
    return jnp.where(((rest >> 2) & 3) == frame, weight, 0.0).astype(BF16)


def norm_kernel(
    place_ref, left_ref, own_ref, right_ref, keys_ref, query_ref, key_scale_ref, query_scale_ref, bias_ref, hidden_ref
):
    ty, tx = place_ref[0], place_ref[1]
    patch = jnp.concatenate([left_ref[...], own_ref[...], right_ref[...]], axis=0)

    def scale_of(field):
        wide = field.astype(F32)
        return lax.rsqrt(jnp.sum(wide * wide, axis=1, keepdims=True) * (1.0 / WIDTH) + 1e-06)

    token = lax.broadcasted_iota(jnp.int32, (256, PATCH), 0)
    for frame in range(4):
        matrix = patch_matrix(frame, (token >> 4) - R, (token & 15) - R, 256, ty, tx)
        rows = slice(frame * 256, (frame + 1) * 256)
        keys_ref[rows, :] = matrix
        field = jnp.dot(matrix, patch, preferred_element_type=F32).astype(BF16)
        key_scale_ref[rows, :] = jnp.broadcast_to(scale_of(field), (256, LANES))
    matrix = patch_matrix(token >> 6, (token >> 3) & 7, token & 7, 256, ty, tx)
    query_ref[...] = matrix
    hidden = jnp.dot(matrix, patch, preferred_element_type=F32).astype(BF16)
    hidden_ref[...] = hidden
    query_scale_ref[...] = jnp.broadcast_to(scale_of(hidden), (256, LANES))
    place = lax.broadcasted_iota(jnp.int32, (1024, LANES), 0)
    row = ((place >> 4) & 15) - R
    col = (place & 15) - R
    allowed = (
        (row + 8 * ty >= 0)
        & (row + 8 * ty < 64)
        & (row >= -place_ref[2])
        & (row < 8 + place_ref[3])
        & (col + 8 * tx >= 0)
        & (col + 8 * tx < 128)
        & (col >= -place_ref[4])
        & (col < 8 + place_ref[5])
    )
    lane = lax.broadcasted_iota(jnp.int32, (1024, LANES), 1)
    bias_ref[...] = jnp.where(((lane & (HD - 1)) == 0) & ~allowed, NEG, 0.0)


def attend_kernel(
    left_ref, own_ref, right_ref, keys_ref, query_ref, key_scale_ref, query_scale_ref, bias_ref, out_ref
):
    patch = jnp.concatenate([left_ref[0], own_ref[0], right_ref[0]], axis=0)
    fine = jnp.dot(keys_ref[...], patch, preferred_element_type=F32)
    query = jnp.dot(query_ref[...], patch, preferred_element_type=F32)
    scale = key_scale_ref[...]
    query_scale = query_scale_ref[...] * (HD ** (-0.5) * 1.4426950408889634)
    bias = bias_ref[...]
    low = lax.broadcasted_iota(jnp.int32, (1024, LANES), 1) < HD
    lane = lax.broadcasted_iota(jnp.int32, (256, LANES), 1)
    query_low = lane < HD
    scores = []
    values = []
    for pair in range(2):
        start = pair * 384
        first = fine[:, start : start + 128] * scale
        second = fine[:, start + 128 : start + 256] * scale
        third = fine[:, start + 256 : start + 384] * scale
        turned_0 = pltpu.roll(query[:, start : start + 128] * query_scale, HD, 1)
        turned_1 = pltpu.roll(query[:, start + 128 : start + 256] * query_scale, HD, 1)
        query_0 = jnp.where(query_low, jnp.where(lane == 0, 1.0, 0.0), turned_0)
        query_1 = jnp.where(query_low, turned_1, jnp.where(lane == HD, 1.0, 0.0))
        key_0 = jnp.where(low, bias, first)
        key_1 = jnp.where(low, third, bias)
        for q, k in ((query_0, key_0), (query_1, key_1)):
            scores.append(
                lax.dot_general(
                    q.astype(BF16), k.astype(BF16), (((1,), (1,)), ((), ())), preferred_element_type=F32
                )
            )
        values.append(jnp.where(low, second, 1.0).astype(BF16))
        values.append(jnp.where(low, 1.0, third).astype(BF16))
    mixed = []
    for score, value in zip(scores, values):
        weights = jnp.exp2(score - jnp.max(score, axis=1, keepdims=True)).astype(BF16)
        mixed.append(jnp.dot(weights, value, preferred_element_type=F32))
    for pair in range(2):
        head_0, head_1 = mixed[2 * pair], mixed[2 * pair + 1]
        both = jnp.where(query_low, head_0 / head_0[:, HD : HD + 1], head_1 / head_1[:, 0:1])
        out_ref[0, :, pair * LANES : (pair + 1) * LANES] = both.astype(BF16)


def output_kernel(place_ref, attended_ref, hidden_ref, w0_ref, w1_ref, w2_ref, w3_ref, out_ref):
    rep = place_ref[0]
    weights = (w0_ref, w1_ref, w2_ref, w3_ref)
    groups = [attended_ref[rep ^ k] for k in range(4)]
    chunks = []
    for t in range(0, CHUNKS, 2):
        total = hidden_ref[:, t * LANES : (t + 2) * LANES].astype(F32)
        for k in range(4):
            pair = jnp.concatenate([weights[k][t], weights[k][t + 1]], axis=1)
            total = total + jnp.dot(groups[k], pair, preferred_element_type=F32)
        chunks.append(total[:, 0:LANES])
        chunks.append(total[:, LANES : 2 * LANES])
    lane = lax.broadcasted_iota(jnp.int32, (256, LANES), 1)
    for j in range(15):
        here, shift = chunks[j], (LANES - 8 * j) % LANES
        if shift:
            here = pltpu.roll(here, shift, 1)
        after = pltpu.roll(chunks[j + 1], CHUNK - 8 * j, 1)
        out_ref[:, j * LANES : (j + 1) * LANES] = jnp.where(lane < CHUNK - 8 * j, here, after).astype(BF16)


def body(latent, in_weight, qkv_weight, out_weight, norm_gain, extents):
    ty = lax.axis_index("ty")
    tx = lax.axis_index("tx")
    rep = lax.axis_index("rep")
    smem = pl.BlockSpec(memory_space=pltpu.SMEM)

    vmem = pl.BlockSpec(memory_space=pltpu.VMEM)
    hbm = pl.BlockSpec(memory_space=pltpu.HBM)
    message, shard = call(
        start_kernel,
        [jax.ShapeDtypeStruct((16, 120, LANES), BF16), jax.ShapeDtypeStruct((176, 768), BF16)],
        58,
        10,
        500,
        in_specs=[smem] + [hbm] * 4,
        out_specs=[vmem, vmem],
        scratch_shapes=[
            pltpu.VMEM(latent.shape, BF16),
            pltpu.VMEM(in_weight.shape, BF16),
            pltpu.VMEM(qkv_weight.shape, BF16),
            pltpu.VMEM((CHUNK, 256), BF16),
            pltpu.SemaphoreType.DMA((4,)),
        ],
    )(ty.astype(jnp.int32).reshape(1), latent, in_weight, qkv_weight, out_weight.T)
    gathered = lax.all_gather(shard, "tx", axis=0)
    moved = lax.all_to_all(message, "tx", split_axis=0, concat_axis=0, tiled=True)
    cells = call(spread_kernel, jax.ShapeDtypeStruct((8, 64, 768), BF16), 16, 10, 1500)(moved)
    cells = lax.all_to_all(cells, "ty", split_axis=0, concat_axis=0, tiled=True)
    sums = call(bridge_kernel, jax.ShapeDtypeStruct((4, 8, 3, 16, 256), BF16), 16, 800, 2000)(
        cells.reshape(512, 768), moved
    )
    parts = lax.all_to_all(
        sums.reshape(32, CELLS, 256), ("rep", "ty"), split_axis=0, concat_axis=0, tiled=True
    )
    gain = jnp.pad(norm_gain.astype(F32).reshape(CHUNKS, CHUNK), ((0, 0), (0, LANES - CHUNK))).reshape(1, WIDE)
    coarse, gained = call(
        reduce_kernel, [jax.ShapeDtypeStruct((CELLS, WIDE), BF16)] * 2, 16, 100, 2000
    )(parts, gain)

    count = lax.axis_size("tx")
    to_right = [(i, i + 1) for i in range(count - 1)]
    to_left = [(i + 1, i) for i in range(count - 1)]
    coarse_left = lax.ppermute(coarse, "tx", to_right)
    coarse_right = lax.ppermute(coarse, "tx", to_left)
    gained = lax.all_gather(gained, "rep", axis=0, tiled=True)
    place = jnp.concatenate([jnp.stack([ty, tx]).astype(jnp.int32), extents.reshape(4)])
    keys, query, key_scale, query_scale, bias, hidden = call(
        norm_kernel,
        [
            jax.ShapeDtypeStruct((1024, PATCH), BF16),
            jax.ShapeDtypeStruct((256, PATCH), BF16),
            jax.ShapeDtypeStruct((1024, LANES), F32),
            jax.ShapeDtypeStruct((256, LANES), F32),
            jax.ShapeDtypeStruct((1024, LANES), F32),
            jax.ShapeDtypeStruct((256, WIDE), BF16),
        ],
        32,
        2000,
        8000,
        in_specs=[smem, vmem, vmem, vmem],
        out_specs=[vmem] * 6,
    )(place, coarse_left, coarse, coarse_right)

    anywhere = pl.BlockSpec(memory_space=pl.ANY)
    project = call(
        project_kernel,
        jax.ShapeDtypeStruct((4 * CELLS, 768), BF16),
        57,
        1000,
        6000,
        in_specs=[vmem, hbm],
        out_specs=vmem,
        scratch_shapes=[pltpu.VMEM((CHUNKS, LANES, 768), BF16), pltpu.SemaphoreType.DMA((4,))],
    )(gained, gathered)
    own_rows = call(
        rows_kernel,
        jax.ShapeDtypeStruct((CHUNKS, 256, LANES), BF16),
        57,
        3000,
        3000,
        in_specs=[hbm, anywhere],
        out_specs=vmem,
        scratch_shapes=[pltpu.VMEM((CHUNKS, 48, 768), BF16), pltpu.SemaphoreType.DMA],
    )(gathered, project)
    project = lax.all_to_all(
        project.reshape(4, CELLS, 768), "rep", split_axis=0, concat_axis=0, tiled=True
    )
    project_left = lax.ppermute(project, "tx", to_right)
    project_right = lax.ppermute(project, "tx", to_left)

    near_rows = lax.ppermute(own_rows, "rep", [(i, i ^ 1) for i in range(4)])
    far_rows = lax.ppermute(own_rows, "rep", [(i, i ^ 2) for i in range(4)])
    last_rows = lax.ppermute(
        own_rows, ("rep", "ty"), [(r * 8 + y, (r ^ 3) * 8 + (y ^ 4)) for r in range(4) for y in range(8)]
    )

    def whole(shape):
        return pl.BlockSpec(shape, lambda p: (0, 0))

    piece = pl.BlockSpec((1, CELLS, 768), lambda p: (p, 0, 0))
    attended = call(
        attend_kernel,
        jax.ShapeDtypeStruct((4, 256, 256), BF16),
        48,
        8000,
        1000,
        grid=(4,),
        in_specs=[
            piece,
            piece,
            piece,
            whole((1024, PATCH)),
            whole((256, PATCH)),
            whole((1024, LANES)),
            whole((256, LANES)),
            whole((1024, LANES)),
        ],
        out_specs=pl.BlockSpec((1, 256, 256), lambda p: (p, 0, 0)),
    )(project_left, project, project_right, keys, query, key_scale, query_scale, bias)

    result = call(
        output_kernel,
        jax.ShapeDtypeStruct((256, WIDTH), BF16),
        32,
        1000,
        6000,
        in_specs=[smem] + [vmem] * 6,
        out_specs=vmem,
    )(rep.astype(jnp.int32).reshape(1), attended, hidden, own_rows, near_rows, far_rows, last_rows)
    return result.reshape(4, 8, 8, WIDTH)


def solution(mesh):
    return jax.shard_map(
        body,
        mesh=mesh,
        in_specs=(
            P("tx", "ty", None, "rep"),
            P(("rep", "tx"), None),
            P("tx", "rep"),
            P("rep", "tx"),
            P(),
            P("ty", "tx", None),
        ),
        out_specs=P("rep", "ty", "tx", None),
        check_vma=False,
    )
```

```python
import jax
import jax.numpy as jnp
from jax import lax
from jax.experimental import pallas as pl
from jax.experimental.pallas import tpu as pltpu
from jax.sharding import PartitionSpec as P

HD = 64
U = 4
R = 4
CHUNKS = 16
CHUNK = 120
LANES = 128
WIDE = CHUNKS * LANES
WIDTH = CHUNKS * CHUNK
CELLS = 48
PATCH = 3 * CELLS
NEG = -1e30
F32 = jnp.float32
BF16 = jnp.bfloat16


def call(kernel, out_shape, vmem_mb, mflops, kbytes, **kw):
    return pl.pallas_call(
        kernel,
        out_shape=out_shape,
        compiler_params=pltpu.CompilerParams(vmem_limit_bytes=vmem_mb << 20),
        cost_estimate=pl.CostEstimate(flops=mflops * 10**6, bytes_accessed=kbytes * 1000, transcendentals=0),
        **kw,
    )


def start_kernel(
    place_ref, latent_hbm, weight_hbm, qkv_hbm, out_weight_hbm, message_ref, shard_ref, latent_ref, weight_ref, qkv_ref, out_weight_ref, sems
):
    copies = [
        pltpu.make_async_copy(source, target, sems.at[i])
        for i, (source, target) in enumerate(
            (
                (out_weight_hbm, out_weight_ref),
                (qkv_hbm, qkv_ref),
                (weight_hbm, weight_ref),
                (latent_hbm, latent_ref),
            )
        )
    ]
    for copy in copies:
        copy.start()
    copies[0].wait()
    rows = out_weight_ref[...].astype(F32)
    rows = jnp.concatenate([rows, jnp.zeros((LANES - CHUNK, 256), F32)], axis=0).T
    rows = jnp.concatenate([rows, jnp.zeros((32, LANES), F32)], axis=0)
    rows = jnp.concatenate([rows[b * 48 : (b + 1) * 48] for b in range(6)], axis=1)
    shard_ref[128:176, :] = rows.astype(BF16)
    copies[1].wait()
    shard_ref[0:128, :] = jnp.concatenate([qkv_ref[...], jnp.zeros((8, 768), BF16)], axis=0)
    copies[2].wait()
    weight = weight_ref[...].astype(F32)
    block = slice_of(weight, 0)
    for ty in range(1, 8):
        block = jnp.where(place_ref[0] == ty, slice_of(weight, ty), block)
    chunks = [block[:, 0:LANES], block[:, LANES : 2 * LANES]]
    copies[3].wait()
    latent = latent_ref[0].astype(F32)
    for t in range(16):
        cells = jnp.concatenate([latent[0, 2 * t : 2 * t + 2], latent[1, 2 * t : 2 * t + 2]], axis=0)
        cells = [cells[:, b * LANES : (b + 1) * LANES] for b in range(6)]
        message_ref[t] = jnp.concatenate(chunks + cells, axis=0).astype(BF16)


def slice_of(rows, ty):
    lane = lax.broadcasted_iota(jnp.int32, (rows.shape[0], LANES), 1)
    chunks = []
    for t in (2 * ty, 2 * ty + 1):
        tile, shift = divmod(t * CHUNK, LANES)
        first = rows[:, tile * LANES : (tile + 1) * LANES]
        if shift:
            first = pltpu.roll(first, LANES - shift, 1)
        if shift > LANES - CHUNK:
            second = rows[:, (tile + 1) * LANES : (tile + 2) * LANES]
            second = pltpu.roll(second, LANES - shift, 1)
            first = jnp.where(lane < LANES - shift, first, second)
        chunks.append(jnp.where(lane < CHUNK, first, 0.0))
    return jnp.concatenate(chunks, axis=1)


def spread_kernel(moved_ref, out_ref):
    cells = moved_ref[:, 96:120, :].astype(F32)
    cells = jnp.concatenate(
        [cells[:, b * 4 : b * 4 + 4, :].reshape(64, LANES) for b in range(6)], axis=1
    ).astype(BF16)
    for ty in range(8):
        out_ref[ty] = cells


def bridge_kernel(cells_ref, moved_ref, out_ref):
    weight = jnp.concatenate(
        [moved_ref[:, c * 48 : c * 48 + 48, :].reshape(768, LANES) for c in range(2)], axis=1
    )
    sums = jnp.dot(cells_ref[...], weight, preferred_element_type=F32).astype(BF16)
    for y in range(8):
        for dy in range(3):
            source = min(max(y + dy - 1, 0), 7)
            for r in range(4):
                start = source * 64 + r * 16
                out_ref[r, y, dy] = sums[start : start + 16, :]


def reduce_kernel(parts_ref, gain_ref, coarse_ref, gained_ref):
    for y in range(8):
        total = parts_ref[y].astype(F32)
        for r in range(1, 4):
            total = total + parts_ref[r * 8 + y].astype(F32)
        lanes = slice(y * 256, (y + 1) * 256)
        coarse_ref[:, lanes] = total.astype(BF16)
        gained_ref[:, lanes] = (total * gain_ref[:, lanes]).astype(BF16)


def project_kernel(gained_ref, shards_hbm, project_ref, weights_ref, sems):
    copies = []
    for k in range(4):
        part = pl.ds(4 * k, 4)
        copies.append(
            pltpu.make_async_copy(shards_hbm.at[part, pl.ds(0, LANES), :], weights_ref.at[part], sems.at[k])
        )
        copies[k].start()
    total = jnp.zeros(project_ref.shape, F32)
    for k in range(4):
        copies[k].wait()
        total = total + jnp.dot(
            gained_ref[:, k * 512 : (k + 1) * 512],
            weights_ref[4 * k : 4 * k + 4].reshape(512, 768),
            preferred_element_type=F32,
        )
    project_ref[...] = total.astype(BF16)


def rows_kernel(weights_hbm, after_ref, out_ref, weights_ref, sems):
    copies = []
    for k in range(4):
        part = pl.ds(4 * k, 4)
        copies.append(
            pltpu.make_async_copy(weights_hbm.at[part, pl.ds(LANES, 48), :], weights_ref.at[part], sems.at[k])
        )
        copies[k].start()
    for t in range(CHUNKS):
        if t % 4 == 0:
            copies[t // 4].wait()
        for b in range(6):
            rows = 48 if b < 5 else 16
            out_ref[t, b * 48 : b * 48 + rows, :] = weights_ref[t, 0:rows, b * LANES : (b + 1) * LANES]


def axis_weight(fine, cell, low, high):
    near = ((fine + 4) >> 2) - 1
    offset = ((fine + 4) & 3).astype(F32) * 0.25 - 0.375
    before = jnp.clip(near - 1, low, high)
    after = jnp.clip(near + 1, low, high)
    return (
        jnp.where(cell == near, 1.0 - jnp.abs(offset), 0.0)
        + jnp.where(cell == before, jnp.maximum(-offset, 0.0), 0.0)
        + jnp.where(cell == after, jnp.maximum(offset, 0.0), 0.0)
    )


def patch_matrix(frame, fine_row, fine_col, tokens, ty, tx):
    lane = lax.broadcasted_iota(jnp.int32, (tokens, PATCH), 1)
    piece = (lane >= CELLS).astype(jnp.int32) + (lane >= 2 * CELLS).astype(jnp.int32)
    rest = lane - piece * CELLS
    row = ((rest >> 4) << 1) + ((rest >> 1) & 1) - 2
    col = (piece << 1) + (rest & 1) - 2
    weight = axis_weight(fine_row, row, -2 * ty, 15 - 2 * ty) * axis_weight(
        fine_col, col, -2 * tx, 31 - 2 * tx
    )
    return jnp.where(((rest >> 2) & 3) == frame, weight, 0.0).astype(BF16)


def norm_kernel(
    place_ref, left_ref, own_ref, right_ref, keys_ref, query_ref, key_scale_ref, query_scale_ref, bias_ref, hidden_ref
):
    ty, tx = place_ref[0], place_ref[1]
    patch = jnp.concatenate([left_ref[...], own_ref[...], right_ref[...]], axis=0)

    def scale_of(field):
        wide = field.astype(F32)
        return lax.rsqrt(jnp.sum(wide * wide, axis=1, keepdims=True) * (1.0 / WIDTH) + 1e-06)

    token = lax.broadcasted_iota(jnp.int32, (256, PATCH), 0)
    for frame in range(4):
        matrix = patch_matrix(frame, (token >> 4) - R, (token & 15) - R, 256, ty, tx)
        rows = slice(frame * 256, (frame + 1) * 256)
        keys_ref[rows, :] = matrix
        field = jnp.dot(matrix, patch, preferred_element_type=F32).astype(BF16)
        key_scale_ref[rows, :] = jnp.broadcast_to(scale_of(field), (256, LANES))
    matrix = patch_matrix(token >> 6, (token >> 3) & 7, token & 7, 256, ty, tx)
    query_ref[...] = matrix
    hidden = jnp.dot(matrix, patch, preferred_element_type=F32).astype(BF16)
    hidden_ref[...] = hidden
    query_scale_ref[...] = jnp.broadcast_to(scale_of(hidden), (256, LANES))
    place = lax.broadcasted_iota(jnp.int32, (1024, LANES), 0)
    row = ((place >> 4) & 15) - R
    col = (place & 15) - R
    allowed = (
        (row + 8 * ty >= 0)
        & (row + 8 * ty < 64)
        & (row >= -place_ref[2])
        & (row < 8 + place_ref[3])
        & (col + 8 * tx >= 0)
        & (col + 8 * tx < 128)
        & (col >= -place_ref[4])
        & (col < 8 + place_ref[5])
    )
    lane = lax.broadcasted_iota(jnp.int32, (1024, LANES), 1)
    bias_ref[...] = jnp.where(((lane & (HD - 1)) == 0) & ~allowed, NEG, 0.0)


def attend_kernel(
    left_ref, own_ref, right_ref, keys_ref, query_ref, key_scale_ref, query_scale_ref, bias_ref, out_ref
):
    patch = jnp.concatenate([left_ref[0], own_ref[0], right_ref[0]], axis=0)
    fine = jnp.dot(keys_ref[...], patch, preferred_element_type=F32)
    query = jnp.dot(query_ref[...], patch, preferred_element_type=F32)
    scale = key_scale_ref[...]
    query_scale = query_scale_ref[...] * (HD ** (-0.5) * 1.4426950408889634)
    bias = bias_ref[...]
    low = lax.broadcasted_iota(jnp.int32, (1024, LANES), 1) < HD
    lane = lax.broadcasted_iota(jnp.int32, (256, LANES), 1)
    query_low = lane < HD
    heads = []
    for pair in range(2):
        start = pair * 384
        first = fine[:, start : start + 128] * scale
        second = fine[:, start + 128 : start + 256] * scale
        third = fine[:, start + 256 : start + 384] * scale
        turned_0 = pltpu.roll(query[:, start : start + 128] * query_scale, HD, 1)
        turned_1 = pltpu.roll(query[:, start + 128 : start + 256] * query_scale, HD, 1)
        query_0 = jnp.where(query_low, jnp.where(lane == 0, 1.0, 0.0), turned_0).astype(BF16)
        query_1 = jnp.where(query_low, turned_1, jnp.where(lane == HD, 1.0, 0.0)).astype(BF16)
        key_0 = jnp.where(low, bias, first).astype(BF16)
        key_1 = jnp.where(low, third, bias).astype(BF16)
        value_0 = jnp.where(low, second, 1.0).astype(BF16)
        value_1 = jnp.where(low, 1.0, third).astype(BF16)
        heads += [(query_0, key_0, value_0), (query_1, key_1, value_1)]
    block_low = query_low[0:128]
    for start in (0, 128):
        rows = slice(start, start + 128)
        scores = [
            lax.dot_general(q[rows], k, (((1,), (1,)), ((), ())), preferred_element_type=F32) for q, k, _ in heads
        ]
        mixed = []
        for score, (_, _, value) in zip(scores, heads):
            weights = jnp.exp2(score - jnp.max(score, axis=1, keepdims=True)).astype(BF16)
            mixed.append(jnp.dot(weights, value, preferred_element_type=F32))
        for pair in range(2):
            head_0, head_1 = mixed[2 * pair], mixed[2 * pair + 1]
            both = jnp.where(block_low, head_0 / head_0[:, HD : HD + 1], head_1 / head_1[:, 0:1])
            out_ref[0, rows, pair * LANES : (pair + 1) * LANES] = both.astype(BF16)


def output_kernel(place_ref, attended_ref, hidden_ref, w0_ref, w1_ref, w2_ref, w3_ref, out_ref):
    rep = place_ref[0]
    weights = (w0_ref, w1_ref, w2_ref, w3_ref)
    groups = [attended_ref[rep ^ k] for k in range(4)]
    chunks = []
    for t in range(0, CHUNKS, 2):
        total = hidden_ref[:, t * LANES : (t + 2) * LANES].astype(F32)
        for k in range(4):
            pair = jnp.concatenate([weights[k][t], weights[k][t + 1]], axis=1)
            total = total + jnp.dot(groups[k], pair, preferred_element_type=F32)
        chunks.append(total[:, 0:LANES])
        chunks.append(total[:, LANES : 2 * LANES])
    lane = lax.broadcasted_iota(jnp.int32, (256, LANES), 1)
    for j in range(15):
        here, shift = chunks[j], (LANES - 8 * j) % LANES
        if shift:
            here = pltpu.roll(here, shift, 1)
        after = pltpu.roll(chunks[j + 1], CHUNK - 8 * j, 1)
        out_ref[:, j * LANES : (j + 1) * LANES] = jnp.where(lane < CHUNK - 8 * j, here, after).astype(BF16)


def body(latent, in_weight, qkv_weight, out_weight, norm_gain, extents):
    ty = lax.axis_index("ty")
    tx = lax.axis_index("tx")
    rep = lax.axis_index("rep")
    smem = pl.BlockSpec(memory_space=pltpu.SMEM)

    vmem = pl.BlockSpec(memory_space=pltpu.VMEM)
    hbm = pl.BlockSpec(memory_space=pltpu.HBM)
    message, shard = call(
        start_kernel,
        [jax.ShapeDtypeStruct((16, 120, LANES), BF16), jax.ShapeDtypeStruct((176, 768), BF16)],
        58,
        10,
        500,
        in_specs=[smem] + [hbm] * 4,
        out_specs=[vmem, vmem],
        scratch_shapes=[
            pltpu.VMEM(latent.shape, BF16),
            pltpu.VMEM(in_weight.shape, BF16),
            pltpu.VMEM(qkv_weight.shape, BF16),
            pltpu.VMEM((CHUNK, 256), BF16),
            pltpu.SemaphoreType.DMA((4,)),
        ],
    )(ty.astype(jnp.int32).reshape(1), latent, in_weight, qkv_weight, out_weight.T)
    gathered = lax.all_gather(shard, "tx", axis=0)
    moved = lax.all_to_all(message, "tx", split_axis=0, concat_axis=0, tiled=True)
    cells = call(spread_kernel, jax.ShapeDtypeStruct((8, 64, 768), BF16), 16, 10, 1500)(moved)
    cells = lax.all_to_all(cells, "ty", split_axis=0, concat_axis=0, tiled=True)
    sums = call(bridge_kernel, jax.ShapeDtypeStruct((4, 8, 3, 16, 256), BF16), 16, 800, 2000)(
        cells.reshape(512, 768), moved
    )
    parts = lax.all_to_all(
        sums.reshape(32, CELLS, 256), ("rep", "ty"), split_axis=0, concat_axis=0, tiled=True
    )
    gain = jnp.pad(norm_gain.astype(F32).reshape(CHUNKS, CHUNK), ((0, 0), (0, LANES - CHUNK))).reshape(1, WIDE)
    coarse, gained = call(
        reduce_kernel, [jax.ShapeDtypeStruct((CELLS, WIDE), BF16)] * 2, 16, 100, 2000
    )(parts, gain)

    count = lax.axis_size("tx")
    to_right = [(i, i + 1) for i in range(count - 1)]
    to_left = [(i + 1, i) for i in range(count - 1)]
    coarse_left = lax.ppermute(coarse, "tx", to_right)
    coarse_right = lax.ppermute(coarse, "tx", to_left)
    gained = lax.all_gather(gained, "rep", axis=0, tiled=True)
    place = jnp.concatenate([jnp.stack([ty, tx]).astype(jnp.int32), extents.reshape(4)])
    keys, query, key_scale, query_scale, bias, hidden = call(
        norm_kernel,
        [
            jax.ShapeDtypeStruct((1024, PATCH), BF16),
            jax.ShapeDtypeStruct((256, PATCH), BF16),
            jax.ShapeDtypeStruct((1024, LANES), F32),
            jax.ShapeDtypeStruct((256, LANES), F32),
            jax.ShapeDtypeStruct((1024, LANES), F32),
            jax.ShapeDtypeStruct((256, WIDE), BF16),
        ],
        32,
        2000,
        8000,
        in_specs=[smem, vmem, vmem, vmem],
        out_specs=[vmem] * 6,
    )(place, coarse_left, coarse, coarse_right)

    anywhere = pl.BlockSpec(memory_space=pl.ANY)
    project = call(
        project_kernel,
        jax.ShapeDtypeStruct((4 * CELLS, 768), BF16),
        57,
        1000,
        6000,
        in_specs=[vmem, hbm],
        out_specs=vmem,
        scratch_shapes=[pltpu.VMEM((CHUNKS, LANES, 768), BF16), pltpu.SemaphoreType.DMA((4,))],
    )(gained, gathered)
    own_rows = call(
        rows_kernel,
        jax.ShapeDtypeStruct((CHUNKS, 256, LANES), BF16),
        57,
        3000,
        3000,
        in_specs=[hbm, anywhere],
        out_specs=vmem,
        scratch_shapes=[pltpu.VMEM((CHUNKS, 48, 768), BF16), pltpu.SemaphoreType.DMA((4,))],
    )(gathered, project)
    project = lax.all_to_all(
        project.reshape(4, CELLS, 768), "rep", split_axis=0, concat_axis=0, tiled=True
    )
    project_left = lax.ppermute(project, "tx", to_right)
    project_right = lax.ppermute(project, "tx", to_left)

    near_rows = lax.ppermute(own_rows, "rep", [(i, i ^ 1) for i in range(4)])
    far_rows = lax.ppermute(own_rows, "rep", [(i, i ^ 2) for i in range(4)])
    last_rows = lax.ppermute(
        own_rows, ("rep", "ty"), [(r * 8 + y, (r ^ 3) * 8 + (y ^ 4)) for r in range(4) for y in range(8)]
    )

    def whole(shape):
        return pl.BlockSpec(shape, lambda p: (0, 0))

    piece = pl.BlockSpec((1, CELLS, 768), lambda p: (p, 0, 0))
    attended = call(
        attend_kernel,
        jax.ShapeDtypeStruct((4, 256, 256), BF16),
        48,
        8000,
        1000,
        grid=(4,),
        in_specs=[
            piece,
            piece,
            piece,
            whole((1024, PATCH)),
            whole((256, PATCH)),
            whole((1024, LANES)),
            whole((256, LANES)),
            whole((1024, LANES)),
        ],
        out_specs=pl.BlockSpec((1, 256, 256), lambda p: (p, 0, 0)),
    )(project_left, project, project_right, keys, query, key_scale, query_scale, bias)

    result = call(
        output_kernel,
        jax.ShapeDtypeStruct((256, WIDTH), BF16),
        32,
        1000,
        6000,
        in_specs=[smem] + [vmem] * 6,
        out_specs=vmem,
    )(rep.astype(jnp.int32).reshape(1), attended, hidden, own_rows, near_rows, far_rows, last_rows)
    return result.reshape(4, 8, 8, WIDTH)


def solution(mesh):
    return jax.shard_map(
        body,
        mesh=mesh,
        in_specs=(
            P("tx", "ty", None, "rep"),
            P(("rep", "tx"), None),
            P("tx", "rep"),
            P("rep", "tx"),
            P(),
            P("ty", "tx", None),
        ),
        out_specs=P("rep", "ty", "tx", None),
        check_vma=False,
    )
```

```python
import jax
import jax.numpy as jnp
from jax import lax
from jax.experimental import pallas as pl
from jax.experimental.pallas import tpu as pltpu
from jax.sharding import PartitionSpec as P

HD = 64
U = 4
R = 4
CHUNKS = 16
CHUNK = 120
LANES = 128
WIDE = CHUNKS * LANES
WIDTH = CHUNKS * CHUNK
CELLS = 48
PATCH = 3 * CELLS
NEG = -1e30
F32 = jnp.float32
BF16 = jnp.bfloat16


def call(kernel, out_shape, vmem_mb, mflops, kbytes, **kw):
    return pl.pallas_call(
        kernel,
        out_shape=out_shape,
        compiler_params=pltpu.CompilerParams(vmem_limit_bytes=vmem_mb << 20),
        cost_estimate=pl.CostEstimate(flops=mflops * 10**6, bytes_accessed=kbytes * 1000, transcendentals=0),
        **kw,
    )


def start_kernel(
    place_ref, latent_hbm, weight_hbm, qkv_hbm, out_weight_hbm, message_ref, shard_ref, latent_ref, weight_ref, qkv_ref, out_weight_ref, sems
):
    copies = [
        pltpu.make_async_copy(source, target, sems.at[i])
        for i, (source, target) in enumerate(
            (
                (out_weight_hbm, out_weight_ref),
                (qkv_hbm, qkv_ref),
                (weight_hbm, weight_ref),
                (latent_hbm, latent_ref),
            )
        )
    ]
    for copy in copies:
        copy.start()
    copies[0].wait()
    rows = out_weight_ref[...].astype(F32)
    rows = jnp.concatenate([rows, jnp.zeros((LANES - CHUNK, 256), F32)], axis=0).T
    rows = jnp.concatenate([rows, jnp.zeros((32, LANES), F32)], axis=0)
    rows = jnp.concatenate([rows[b * 48 : (b + 1) * 48] for b in range(6)], axis=1)
    shard_ref[128:176, :] = rows.astype(BF16)
    copies[1].wait()
    shard_ref[0:128, :] = jnp.concatenate([qkv_ref[...], jnp.zeros((8, 768), BF16)], axis=0)
    copies[2].wait()
    weight = weight_ref[...].astype(F32)
    block = slice_of(weight, 0)
    for ty in range(1, 8):
        block = jnp.where(place_ref[0] == ty, slice_of(weight, ty), block)
    chunks = [block[:, 0:LANES], block[:, LANES : 2 * LANES]]
    copies[3].wait()
    latent = latent_ref[0].astype(F32)
    for t in range(16):
        cells = jnp.concatenate([latent[0, 2 * t : 2 * t + 2], latent[1, 2 * t : 2 * t + 2]], axis=0)
        cells = [cells[:, b * LANES : (b + 1) * LANES] for b in range(6)]
        message_ref[t] = jnp.concatenate(chunks + cells, axis=0).astype(BF16)


def slice_of(rows, ty):
    lane = lax.broadcasted_iota(jnp.int32, (rows.shape[0], LANES), 1)
    chunks = []
    for t in (2 * ty, 2 * ty + 1):
        tile, shift = divmod(t * CHUNK, LANES)
        first = rows[:, tile * LANES : (tile + 1) * LANES]
        if shift:
            first = pltpu.roll(first, LANES - shift, 1)
        if shift > LANES - CHUNK:
            second = rows[:, (tile + 1) * LANES : (tile + 2) * LANES]
            second = pltpu.roll(second, LANES - shift, 1)
            first = jnp.where(lane < LANES - shift, first, second)
        chunks.append(jnp.where(lane < CHUNK, first, 0.0))
    return jnp.concatenate(chunks, axis=1)


def spread_kernel(moved_ref, out_ref):
    cells = moved_ref[:, 96:120, :].astype(F32)
    cells = jnp.concatenate(
        [cells[:, b * 4 : b * 4 + 4, :].reshape(64, LANES) for b in range(6)], axis=1
    ).astype(BF16)
    for ty in range(8):
        out_ref[ty] = cells


def bridge_kernel(cells_ref, moved_ref, out_ref):
    weight = jnp.concatenate(
        [moved_ref[:, c * 48 : c * 48 + 48, :].reshape(768, LANES) for c in range(2)], axis=1
    )
    sums = jnp.dot(cells_ref[...], weight, preferred_element_type=F32).astype(BF16)
    for y in range(8):
        for dy in range(3):
            source = min(max(y + dy - 1, 0), 7)
            for r in range(4):
                start = source * 64 + r * 16
                out_ref[r, y, dy] = sums[start : start + 16, :]


def reduce_kernel(parts_ref, gain_ref, coarse_ref, gained_ref):
    for y in range(8):
        total = parts_ref[y].astype(F32)
        for r in range(1, 4):
            total = total + parts_ref[r * 8 + y].astype(F32)
        lanes = slice(y * 256, (y + 1) * 256)
        coarse_ref[:, lanes] = total.astype(BF16)
        gained_ref[:, lanes] = (total * gain_ref[:, lanes]).astype(BF16)


def project_kernel(gained_ref, shards_hbm, project_ref, weights_ref, sems):
    copies = []
    for k in range(4):
        part = pl.ds(4 * k, 4)
        copies.append(
            pltpu.make_async_copy(shards_hbm.at[part, pl.ds(0, LANES), :], weights_ref.at[part], sems.at[k])
        )
        copies[k].start()
    total = jnp.zeros(project_ref.shape, F32)
    for k in range(4):
        copies[k].wait()
        total = total + jnp.dot(
            gained_ref[:, k * 512 : (k + 1) * 512],
            weights_ref[4 * k : 4 * k + 4].reshape(512, 768),
            preferred_element_type=F32,
        )
    project_ref[...] = total.astype(BF16)


def rows_kernel(weights_hbm, after_ref, out_ref, weights_ref, sems):
    copies = []
    for k in range(4):
        part = pl.ds(4 * k, 4)
        copies.append(
            pltpu.make_async_copy(weights_hbm.at[part, pl.ds(LANES, 48), :], weights_ref.at[part], sems.at[k])
        )
        copies[k].start()
    for t in range(CHUNKS):
        if t % 4 == 0:
            copies[t // 4].wait()
        for b in range(6):
            rows = 48 if b < 5 else 16
            out_ref[t, b * 48 : b * 48 + rows, :] = weights_ref[t, 0:rows, b * LANES : (b + 1) * LANES]


def axis_weight(fine, cell, low, high):
    near = ((fine + 4) >> 2) - 1
    offset = ((fine + 4) & 3).astype(F32) * 0.25 - 0.375
    before = jnp.clip(near - 1, low, high)
    after = jnp.clip(near + 1, low, high)
    return (
        jnp.where(cell == near, 1.0 - jnp.abs(offset), 0.0)
        + jnp.where(cell == before, jnp.maximum(-offset, 0.0), 0.0)
        + jnp.where(cell == after, jnp.maximum(offset, 0.0), 0.0)
    )


def patch_matrix(frame, fine_row, fine_col, tokens, ty, tx):
    lane = lax.broadcasted_iota(jnp.int32, (tokens, PATCH), 1)
    piece = (lane >= CELLS).astype(jnp.int32) + (lane >= 2 * CELLS).astype(jnp.int32)
    rest = lane - piece * CELLS
    row = ((rest >> 4) << 1) + ((rest >> 1) & 1) - 2
    col = (piece << 1) + (rest & 1) - 2
    weight = axis_weight(fine_row, row, -2 * ty, 15 - 2 * ty) * axis_weight(
        fine_col, col, -2 * tx, 31 - 2 * tx
    )
    return jnp.where(((rest >> 2) & 3) == frame, weight, 0.0).astype(BF16)


def norm_kernel(
    place_ref, left_ref, own_ref, right_ref, keys_ref, query_ref, key_scale_ref, query_scale_ref, bias_ref, hidden_ref
):
    ty, tx = place_ref[0], place_ref[1]
    patch = jnp.concatenate([left_ref[...], own_ref[...], right_ref[...]], axis=0)

    def scale_of(field):
        wide = field.astype(F32)
        return lax.rsqrt(jnp.sum(wide * wide, axis=1, keepdims=True) * (1.0 / WIDTH) + 1e-06)

    token = lax.broadcasted_iota(jnp.int32, (256, PATCH), 0)
    for frame in range(4):
        matrix = patch_matrix(frame, (token >> 4) - R, (token & 15) - R, 256, ty, tx)
        rows = slice(frame * 256, (frame + 1) * 256)
        keys_ref[rows, :] = matrix
        field = jnp.dot(matrix, patch, preferred_element_type=F32).astype(BF16)
        key_scale_ref[rows, :] = jnp.broadcast_to(scale_of(field), (256, LANES))
    matrix = patch_matrix(token >> 6, (token >> 3) & 7, token & 7, 256, ty, tx)
    query_ref[...] = matrix
    hidden = jnp.dot(matrix, patch, preferred_element_type=F32).astype(BF16)
    hidden_ref[...] = hidden
    query_scale_ref[...] = jnp.broadcast_to(scale_of(hidden), (256, LANES))
    place = lax.broadcasted_iota(jnp.int32, (1024, LANES), 0)
    row = ((place >> 4) & 15) - R
    col = (place & 15) - R
    allowed = (
        (row + 8 * ty >= 0)
        & (row + 8 * ty < 64)
        & (row >= -place_ref[2])
        & (row < 8 + place_ref[3])
        & (col + 8 * tx >= 0)
        & (col + 8 * tx < 128)
        & (col >= -place_ref[4])
        & (col < 8 + place_ref[5])
    )
    lane = lax.broadcasted_iota(jnp.int32, (1024, LANES), 1)
    bias_ref[...] = jnp.where(((lane & (HD - 1)) == 0) & ~allowed, NEG, 0.0)


def attend_kernel(
    left_ref, own_ref, right_ref, keys_ref, query_ref, key_scale_ref, query_scale_ref, bias_ref, out_ref
):
    patch = jnp.concatenate([left_ref[0], own_ref[0], right_ref[0]], axis=0)
    fine = jnp.dot(keys_ref[...], patch, preferred_element_type=F32)
    query = jnp.dot(query_ref[...], patch, preferred_element_type=F32)
    scale = key_scale_ref[...]
    query_scale = query_scale_ref[...] * (HD ** (-0.5) * 1.4426950408889634)
    bias = bias_ref[...]
    low = lax.broadcasted_iota(jnp.int32, (1024, LANES), 1) < HD
    lane = lax.broadcasted_iota(jnp.int32, (256, LANES), 1)
    query_low = lane < HD
    heads = []
    for pair in range(2):
        start = pair * 384
        first = fine[:, start : start + 128] * scale
        second = fine[:, start + 128 : start + 256] * scale
        third = fine[:, start + 256 : start + 384] * scale
        turned_0 = pltpu.roll(query[:, start : start + 128] * query_scale, HD, 1)
        turned_1 = pltpu.roll(query[:, start + 128 : start + 256] * query_scale, HD, 1)
        query_0 = jnp.where(query_low, jnp.where(lane == 0, 1.0, 0.0), turned_0).astype(BF16)
        query_1 = jnp.where(query_low, turned_1, jnp.where(lane == HD, 1.0, 0.0)).astype(BF16)
        key_0 = jnp.where(low, bias, first).astype(BF16)
        key_1 = jnp.where(low, third, bias).astype(BF16)
        value_0 = jnp.where(low, second, 1.0).astype(BF16)
        value_1 = jnp.where(low, 1.0, third).astype(BF16)
        heads += [(query_0, key_0, value_0), (query_1, key_1, value_1)]
    block_low = query_low[0:128]
    for start in (0, 128):
        rows = slice(start, start + 128)
        scores = [
            lax.dot_general(q[rows], k, (((1,), (1,)), ((), ())), preferred_element_type=F32) for q, k, _ in heads
        ]
        mixed = []
        for score, (_, _, value) in zip(scores, heads):
            weights = jnp.exp2(score - jnp.max(score, axis=1, keepdims=True)).astype(BF16)
            mixed.append(jnp.dot(weights, value, preferred_element_type=F32))
        for pair in range(2):
            head_0, head_1 = mixed[2 * pair], mixed[2 * pair + 1]
            both = jnp.where(block_low, head_0 / head_0[:, HD : HD + 1], head_1 / head_1[:, 0:1])
            out_ref[0, rows, pair * LANES : (pair + 1) * LANES] = both.astype(BF16)


def times_rows(group, rows, t):
    pair = jnp.concatenate([rows[t], rows[t + 1]], axis=1)
    return jnp.dot(group, pair, preferred_element_type=F32)


def partial_kernel(place_ref, attended_ref, hidden_ref, w0_ref, w1_ref, out_ref):
    rep = place_ref[0]
    groups = [attended_ref[rep ^ k] for k in (0, 1)]
    for t in range(0, CHUNKS, 2):
        lanes = slice(t * LANES, (t + 2) * LANES)
        total = hidden_ref[:, lanes].astype(F32)
        for group, rows in zip(groups, (w0_ref, w1_ref)):
            total = total + times_rows(group, rows, t)
        out_ref[:, lanes] = total


def output_kernel(place_ref, attended_ref, total_ref, w2_ref, w3_ref, out_ref):
    group_2 = attended_ref[place_ref[0] ^ 2]
    group_3 = attended_ref[place_ref[0] ^ 3]
    chunks = []
    for t in range(0, CHUNKS, 2):
        total = total_ref[:, t * LANES : (t + 2) * LANES] + times_rows(group_2, w2_ref, t)
        total = total + times_rows(group_3, w3_ref, t)
        chunks.append(total[:, 0:LANES])
        chunks.append(total[:, LANES : 2 * LANES])
    lane = lax.broadcasted_iota(jnp.int32, (256, LANES), 1)
    for j in range(15):
        here, shift = chunks[j], (LANES - 8 * j) % LANES
        if shift:
            here = pltpu.roll(here, shift, 1)
        after = pltpu.roll(chunks[j + 1], CHUNK - 8 * j, 1)
        out_ref[:, j * LANES : (j + 1) * LANES] = jnp.where(lane < CHUNK - 8 * j, here, after).astype(BF16)


def body(latent, in_weight, qkv_weight, out_weight, norm_gain, extents):
    ty = lax.axis_index("ty")
    tx = lax.axis_index("tx")
    rep = lax.axis_index("rep")
    smem = pl.BlockSpec(memory_space=pltpu.SMEM)

    vmem = pl.BlockSpec(memory_space=pltpu.VMEM)
    hbm = pl.BlockSpec(memory_space=pltpu.HBM)
    message, shard = call(
        start_kernel,
        [jax.ShapeDtypeStruct((16, 120, LANES), BF16), jax.ShapeDtypeStruct((176, 768), BF16)],
        58,
        10,
        500,
        in_specs=[smem] + [hbm] * 4,
        out_specs=[vmem, vmem],
        scratch_shapes=[
            pltpu.VMEM(latent.shape, BF16),
            pltpu.VMEM(in_weight.shape, BF16),
            pltpu.VMEM(qkv_weight.shape, BF16),
            pltpu.VMEM((CHUNK, 256), BF16),
            pltpu.SemaphoreType.DMA((4,)),
        ],
    )(ty.astype(jnp.int32).reshape(1), latent, in_weight, qkv_weight, out_weight.T)
    gathered = lax.all_gather(shard, "tx", axis=0)
    moved = lax.all_to_all(message, "tx", split_axis=0, concat_axis=0, tiled=True)
    cells = call(spread_kernel, jax.ShapeDtypeStruct((8, 64, 768), BF16), 16, 10, 1500)(moved)
    cells = lax.all_to_all(cells, "ty", split_axis=0, concat_axis=0, tiled=True)
    sums = call(bridge_kernel, jax.ShapeDtypeStruct((4, 8, 3, 16, 256), BF16), 16, 800, 2000)(
        cells.reshape(512, 768), moved
    )
    parts = lax.all_to_all(
        sums.reshape(32, CELLS, 256), ("rep", "ty"), split_axis=0, concat_axis=0, tiled=True
    )
    gain = jnp.pad(norm_gain.astype(F32).reshape(CHUNKS, CHUNK), ((0, 0), (0, LANES - CHUNK))).reshape(1, WIDE)
    coarse, gained = call(
        reduce_kernel, [jax.ShapeDtypeStruct((CELLS, WIDE), BF16)] * 2, 16, 100, 2000
    )(parts, gain)

    count = lax.axis_size("tx")
    to_right = [(i, i + 1) for i in range(count - 1)]
    to_left = [(i + 1, i) for i in range(count - 1)]
    coarse_left = lax.ppermute(coarse, "tx", to_right)
    coarse_right = lax.ppermute(coarse, "tx", to_left)
    gained = lax.all_gather(gained, "rep", axis=0, tiled=True)
    place = jnp.concatenate([jnp.stack([ty, tx]).astype(jnp.int32), extents.reshape(4)])
    keys, query, key_scale, query_scale, bias, hidden = call(
        norm_kernel,
        [
            jax.ShapeDtypeStruct((1024, PATCH), BF16),
            jax.ShapeDtypeStruct((256, PATCH), BF16),
            jax.ShapeDtypeStruct((1024, LANES), F32),
            jax.ShapeDtypeStruct((256, LANES), F32),
            jax.ShapeDtypeStruct((1024, LANES), F32),
            jax.ShapeDtypeStruct((256, WIDE), BF16),
        ],
        32,
        2000,
        8000,
        in_specs=[smem, vmem, vmem, vmem],
        out_specs=[vmem] * 6,
    )(place, coarse_left, coarse, coarse_right)

    anywhere = pl.BlockSpec(memory_space=pl.ANY)
    project = call(
        project_kernel,
        jax.ShapeDtypeStruct((4 * CELLS, 768), BF16),
        57,
        1000,
        6000,
        in_specs=[vmem, hbm],
        out_specs=vmem,
        scratch_shapes=[pltpu.VMEM((CHUNKS, LANES, 768), BF16), pltpu.SemaphoreType.DMA((4,))],
    )(gained, gathered)
    own_rows = call(
        rows_kernel,
        jax.ShapeDtypeStruct((CHUNKS, 256, LANES), BF16),
        57,
        3000,
        3000,
        in_specs=[hbm, anywhere],
        out_specs=vmem,
        scratch_shapes=[pltpu.VMEM((CHUNKS, 48, 768), BF16), pltpu.SemaphoreType.DMA((4,))],
    )(gathered, project)
    project = lax.all_to_all(
        project.reshape(4, CELLS, 768), "rep", split_axis=0, concat_axis=0, tiled=True
    )
    project_left = lax.ppermute(project, "tx", to_right)
    project_right = lax.ppermute(project, "tx", to_left)

    near_rows = lax.ppermute(own_rows, "rep", [(i, i ^ 1) for i in range(4)])
    far_rows = lax.ppermute(own_rows, "rep", [(i, i ^ 2) for i in range(4)])
    last_rows = lax.ppermute(
        own_rows, ("rep", "ty"), [(r * 8 + y, (r ^ 3) * 8 + (y ^ 4)) for r in range(4) for y in range(8)]
    )

    def whole(shape):
        return pl.BlockSpec(shape, lambda p: (0, 0))

    piece = pl.BlockSpec((1, CELLS, 768), lambda p: (p, 0, 0))
    attended = call(
        attend_kernel,
        jax.ShapeDtypeStruct((4, 256, 256), BF16),
        48,
        8000,
        1000,
        grid=(4,),
        in_specs=[
            piece,
            piece,
            piece,
            whole((1024, PATCH)),
            whole((256, PATCH)),
            whole((1024, LANES)),
            whole((256, LANES)),
            whole((1024, LANES)),
        ],
        out_specs=pl.BlockSpec((1, 256, 256), lambda p: (p, 0, 0)),
    )(project_left, project, project_right, keys, query, key_scale, query_scale, bias)

    group = rep.astype(jnp.int32).reshape(1)
    total = call(
        partial_kernel,
        jax.ShapeDtypeStruct((256, WIDE), F32),
        32,
        1000,
        6000,
        in_specs=[smem] + [vmem] * 4,
        out_specs=vmem,
    )(group, attended, hidden, own_rows, near_rows)
    result = call(
        output_kernel,
        jax.ShapeDtypeStruct((256, WIDTH), BF16),
        32,
        300,
        3000,
        in_specs=[smem] + [vmem] * 4,
        out_specs=vmem,
    )(group, attended, total, far_rows, last_rows)
    return result.reshape(4, 8, 8, WIDTH)


def solution(mesh):
    return jax.shard_map(
        body,
        mesh=mesh,
        in_specs=(
            P("tx", "ty", None, "rep"),
            P(("rep", "tx"), None),
            P("tx", "rep"),
            P("rep", "tx"),
            P(),
            P("ty", "tx", None),
        ),
        out_specs=P("rep", "ty", "tx", None),
        check_vma=False,
    )
```
